512 devices in a mesh: seq: 64 (over z_lo, y, core), rep: 8 (over x, z_hi).
Axes of the slice: x: 4, y: 4, z: 16 (z_hi: 2, z_lo: 8; z = z_hi * 8 + z_lo), core: 2. Of those that a mesh axis runs over, the one named last changes fastest.
Arguments:
- query_rows: bfloat16 [8, 4096, 8192], P('rep', 'seq'), may hold values from -5 to 5
- unrotated_keys: bfloat16 [8, 4096, 1024], P('rep', 'seq'), may hold values from -5 to 5
- value_projections: bfloat16 [8, 4096, 1024], P('rep', 'seq'), may hold values from -6 to 6
- lengths: int32 [8], P('rep'), may hold values from 1024 to 4096, as said below
- page_table: int32 [8, 512, 1], P('rep', 'seq'), may hold values from 0 to 7; in each aligned block of 8 rows (0 to 7, 8 to 15, ..., all dimensions but the last counted through in order) at most 2 rows name the same one
Outputs:
- attended: bfloat16 [8, 4096, 8192], P('rep', 'seq')
- restored_pages: bfloat16 [8, 64, 8, 2, 8, 2048], P('rep', 'seq')
The draws below stay inside these ranges and needn't reach their ends.
Inputs may be any that keep to these rules, and one draw needn't show every extreme that they name: `lengths`: the longest request of every draw has exactly 4096 tokens. `page_table`: among the 8 pages of one token shard of a request, no owner is named more than 2 times, and in every draw some owner is named exactly 2 times in some shard.
All inputs are finite; a program needn't handle non-finite values.
Results may differ from the reference program's by a relative error of at most 0.011.
Values may be sent and summed in bfloat16 or wider, within the bound.
A program may use at most 64 MiB of HBM per device.

```python
import math
from functools import partial
import jax
import jax.numpy as jnp
import numpy as np
from jax import lax

QUERY_HEAD_COUNT = 64
KEY_VALUE_HEADS = 8
HEAD_SIZE = 128
PAGE_TOKENS = 8
REQUEST_LENGTH = 4096
REQUEST_COUNT = 8
TOKEN_SHARDS = 64
PAGES = 512
SHARD_PAGES = 8
OWNER_SLOTS = 2
BLK = 512


def draw_unrotated_keys(key, part):
    key = jax.random.fold_in(key, 1)
    sampled_rows = jnp.clip(jax.random.normal(key, (REQUEST_COUNT, REQUEST_LENGTH, KEY_VALUE_HEADS, HEAD_SIZE)), -5.0, 5.0)
    return sampled_rows.reshape(REQUEST_COUNT, REQUEST_LENGTH, KEY_VALUE_HEADS * HEAD_SIZE).astype(jnp.bfloat16)


def draw_query_rows(key, part):
    key = jax.random.fold_in(key, 2)
    sampled_rows = jnp.clip(jax.random.normal(key, (REQUEST_COUNT, REQUEST_LENGTH, KEY_VALUE_HEADS, QUERY_HEAD_COUNT // KEY_VALUE_HEADS, HEAD_SIZE)), -5.0, 5.0)
    return sampled_rows.reshape(REQUEST_COUNT, REQUEST_LENGTH, QUERY_HEAD_COUNT * HEAD_SIZE).astype(jnp.bfloat16)


def draw_lengths(key, part):
    key = jax.random.fold_in(key, 3)
    length_key, longest_key = jax.random.split(key)
    drawn_lengths = jax.random.randint(length_key, (REQUEST_COUNT,), REQUEST_LENGTH // 4, REQUEST_LENGTH + 1)
    longest_at = jax.random.randint(longest_key, (), 0, REQUEST_COUNT)
    return jnp.where(jnp.arange(REQUEST_COUNT, dtype=jnp.int32) == longest_at, REQUEST_LENGTH, drawn_lengths).astype(jnp.int32)


def level_of(stream_key, extent, shards, low, high):
    def one(axis_at, shards_of):
        steps = jax.random.uniform(jax.random.fold_in(jax.random.fold_in(stream_key, 6), axis_at), (shards_of,), jnp.float32, low / len(shards), high / len(shards))
        return jnp.repeat(jnp.exp(steps), extent[axis_at] // shards_of).reshape((-1,) + (1,) * (len(extent) - axis_at - 1))

    level = one(*shards[0])
    for cut in shards[1:]:
        level = level * one(*cut)
    return level


def assign_block(stream_key, own, number, rows, amount, top, bound, skew):
    ranking = jax.random.permutation(stream_key, amount)
    packed, ordinary = portions_of(amount, rows * top, bound, skew, True), portions_of(amount, rows * top, bound, skew, False)
    places = jnp.arange(amount)

    def named(tallies, offset_by):
        used = int((tallies > 0).sum())
        fixed = max(1, used // 4)
        moved = fixed + (places - fixed + offset_by * (used - fixed)) % max(1, amount - fixed)
        return jnp.zeros((amount,), jnp.int32).at[ranking[jnp.where(places < fixed, places, moved)]].set(jnp.asarray(tallies, jnp.int32))

    tallies = jnp.where(number % 4 == 0, named(packed, number // 4), named(ordinary, number - number // 4 - 1))
    mixed = jax.random.permutation(jax.random.fold_in(own, 3), amount)
    giver, sink = mixed[0:amount // 2 * 2:2], mixed[1:amount // 2 * 2:2]
    margin = jnp.minimum(tallies[giver] - 1, bound - tallies[sink]) // 2
    margin = jnp.where((giver == ranking[0]) | (sink == ranking[0]) | (tallies[sink] == 0), 0, jnp.maximum(margin, 0))
    moved = jax.random.randint(jax.random.fold_in(own, 4), (amount // 2,), 0, 1 << 20) % (margin + 1)
    tallies = tallies.at[giver].add(-moved).at[sink].add(moved)
    members = jnp.searchsorted(jnp.cumsum(tallies), jnp.arange(rows * top), side="right").astype(jnp.int32)
    table = members.reshape(top, rows).T
    table = table[jax.random.permutation(jax.random.fold_in(own, 1), rows)]
    offset_by = jax.random.randint(jax.random.fold_in(own, 2), (rows, 1), 0, top)
    return jnp.take_along_axis(table, (jnp.arange(top)[None, :] + offset_by) % top, axis=1)


def portions_of(amount, total, bound, slope, full):
    loads = [(1 << 20) // math.isqrt(standing ** slope) + 1 for standing in range(1, amount + 1)]
    largest = bound if full else min(bound, max(-(-total // amount), total * loads[0] // sum(loads)))
    least = 1 if total - largest >= amount - 1 else 0
    given, surplus = [largest] + [least] * (amount - 1), total - largest - least * (amount - 1)
    while surplus > 0:
        free = [i for i in range(1, amount) if given[i] < largest] or [i for i in range(1, amount) if given[i] < bound]
        mass, left = sum([loads[i] for i in free]), surplus
        for i in free:
            extra = min(bound - given[i], max(1, left * loads[i] // mass), surplus)
            given[i] = given[i] + extra
            surplus = surplus - extra
    return np.array(given)


def centred(rng, dims, spread, reach, pieces=(), held_as=jnp.bfloat16):
    entries = jax.random.normal(rng, dims, jnp.float32) * spread
    if len(pieces) > 0:
        entries = level_of(rng, dims, pieces, -0.22, 0.18) * entries
    return jnp.clip(entries, min=-reach, max=reach).astype(held_as)


def setup_inputs(seed: int = 0) -> dict:
    seeds = jax.random.split(jax.random.key(seed), 6)
    query_rows = draw_query_rows(jax.random.fold_in(seeds[5], 71), 0)
    unrotated_keys = draw_unrotated_keys(jax.random.fold_in(seeds[5], 71), 0)
    value_projections = centred(seeds[2], (REQUEST_COUNT, REQUEST_LENGTH, KEY_VALUE_HEADS * HEAD_SIZE), 1.0, 6.0, ((0, 8), (1, 64)))
    lengths = draw_lengths(jax.random.fold_in(seeds[5], 71), 0)
    page_table_keys = jax.random.split(jax.random.fold_in(seeds[4], 1), REQUEST_COUNT * PAGES // SHARD_PAGES)
    page_table_turns = jax.random.permutation(jax.random.fold_in(seeds[4], 3), REQUEST_COUNT * PAGES // SHARD_PAGES)
    page_table = jax.vmap(lambda own, number: assign_block(jax.random.fold_in(seeds[4], 2), own, number, SHARD_PAGES, REQUEST_COUNT, 1, OWNER_SLOTS, 2))(page_table_keys, page_table_turns).reshape((REQUEST_COUNT, PAGES, 1))
    return dict(query_rows=query_rows, unrotated_keys=unrotated_keys, value_projections=value_projections, lengths=lengths, page_table=page_table)


def rotary_embed(values_in, token_positions):
    halfwidth = HEAD_SIZE // 2
    frequency = jnp.exp(-jnp.arange(halfwidth, dtype=jnp.float32) * (2.0 * math.log(500000.0) / HEAD_SIZE))
    angles = token_positions.astype(jnp.float32)[:, None] * frequency[None, :]
    cosine = jnp.cos(angles)[:, None, :]
    sine_part = jnp.sin(angles)[:, None, :]
    first_half = values_in[..., :halfwidth]
    second_half = values_in[..., halfwidth:]
    return jnp.concatenate([first_half * cosine - second_half * sine_part, second_half * cosine + first_half * sine_part], axis=-1)

def slot_table(owner_ids, owners, capacity):
    targets = jnp.arange(owners, dtype=jnp.int32)
    matches = (owner_ids[None, :, :] == targets[:, None, None]).astype(jnp.int32)
    earlier = jnp.cumsum(matches, axis=-1) - matches
    slot_ids = jnp.arange(capacity, dtype=jnp.int32)
    chosen = (matches[:, :, None, :] == 1) & (earlier[:, :, None, :] == slot_ids[None, None, :, None])
    return chosen.astype(jnp.float32)

def head_attention(head_index, query_block, key_block, value_block, allowed, group_width, score_scale):
    query_head = lax.dynamic_index_in_dim(query_block, head_index, 1, keepdims=False)
    key_head = lax.dynamic_index_in_dim(key_block, head_index // group_width, 1, keepdims=False)
    value_head = lax.dynamic_index_in_dim(value_block, head_index // group_width, 1, keepdims=False)
    scores = jnp.dot(query_head, key_head.T, preferred_element_type=jnp.float32) * score_scale
    scores = jnp.where(allowed, scores, -1e+30)
    largest = lax.optimization_barrier(jnp.max(scores, axis=-1, keepdims=True))
    weights = jnp.where(allowed, jnp.exp(scores - largest), 0.0)
    denominator = lax.optimization_barrier(jnp.sum(weights, axis=-1, keepdims=True))
    return jnp.dot(weights.astype(jnp.bfloat16), value_head, preferred_element_type=jnp.float32) / denominator

def reference(query_rows, unrotated_keys, value_projections, lengths, page_table):
    token_positions = jnp.arange(REQUEST_LENGTH, dtype=jnp.int32)
    group_width = QUERY_HEAD_COUNT // KEY_VALUE_HEADS
    score_scale = 1.0 / math.sqrt(HEAD_SIZE)
    attended_all = []
    every_page = []
    for request_index in range(REQUEST_COUNT):
        length = lengths[request_index]
        rotated_q = rotary_embed(query_rows[request_index].astype(jnp.float32).reshape(REQUEST_LENGTH, QUERY_HEAD_COUNT, HEAD_SIZE), token_positions).astype(jnp.bfloat16)
        rotated_keys = rotary_embed(unrotated_keys[request_index].astype(jnp.float32).reshape(REQUEST_LENGTH, KEY_VALUE_HEADS, HEAD_SIZE), token_positions).astype(jnp.bfloat16)
        value_head_rows = value_projections[request_index].reshape(REQUEST_LENGTH, KEY_VALUE_HEADS, HEAD_SIZE)
        blocks = []
        for block_index in range(REQUEST_LENGTH // BLK):
            finish = (block_index + 1) * BLK
            query_positions = token_positions[block_index * BLK:finish]
            key_positions = token_positions[:finish]
            allowed = (key_positions[None, :] <= query_positions[:, None]) & (key_positions[None, :] < length)
            worker = partial(head_attention, query_block=rotated_q[block_index * BLK:finish], key_block=rotated_keys[:finish], value_block=value_head_rows[:finish], allowed=allowed, group_width=group_width, score_scale=score_scale)
            output = lax.map(worker, jnp.arange(QUERY_HEAD_COUNT, dtype=jnp.int32))
            inside = (query_positions < length)[None, :, None]
            blocks.append(jnp.where(inside, output, 0.0).astype(jnp.bfloat16))
        attended_all.append(jnp.concatenate(blocks, axis=1).transpose(1, 0, 2).reshape(REQUEST_LENGTH, QUERY_HEAD_COUNT * HEAD_SIZE))
        in_length = token_positions < length
        cache_entries = jnp.concatenate([rotated_keys.reshape(REQUEST_LENGTH, KEY_VALUE_HEADS * HEAD_SIZE), value_projections[request_index]], axis=-1)
        cache_entries = jnp.where(in_length[:, None], cache_entries, jnp.zeros_like(cache_entries))
        page_groups = cache_entries.reshape(TOKEN_SHARDS, SHARD_PAGES, PAGE_TOKENS * 2 * KEY_VALUE_HEADS * HEAD_SIZE).astype(jnp.float32)
        chosen = slot_table(page_table[request_index, :, 0].reshape(TOKEN_SHARDS, SHARD_PAGES), REQUEST_COUNT, OWNER_SLOTS)
        placed_pages = jnp.einsum('oscj,sjx->oscx', chosen, page_groups)
        every_page.append(placed_pages.astype(jnp.bfloat16).reshape(REQUEST_COUNT, TOKEN_SHARDS, OWNER_SLOTS, PAGE_TOKENS, 2 * KEY_VALUE_HEADS * HEAD_SIZE))
    return (jnp.stack(attended_all, axis=0), jnp.stack(every_page, axis=2))
```

```python
import functools
import math

import jax
import jax.numpy as jnp
from jax import lax
from jax.experimental import pallas as pl
from jax.experimental.pallas import tpu as pltpu
from jax.sharding import PartitionSpec as P

HEAD = 128
PAGE = 8
SLOTS = 2
SLOT_ROWS = SLOTS * PAGE
Z_HALVES = 2
SCALE = math.log2(math.e) / math.sqrt(HEAD)
MESH = pl.DeviceIdType.MESH
NT = (((1,), (1,)), ((), ()))


def rotary_tables(token_positions):
    halfwidth = HEAD // 2
    frequency = jnp.exp(
        -jnp.arange(halfwidth, dtype=jnp.float32) * (2.0 * math.log(500000.0) / HEAD)
    )
    angles = token_positions.astype(jnp.float32)[:, None] * frequency[None, :]
    cosine, sine = jnp.cos(angles), jnp.sin(angles)
    return (
        jnp.concatenate([cosine, cosine], axis=-1),
        jnp.concatenate([-sine, sine], axis=-1),
    )


def kernel(
    groups, zs, xs,
    q_ref, k_ref, v_ref, cos_ref, sin_ref, len_ref, table_ref,
    o_ref, pages_ref,
    kv_out, kv_all, q_out, q_mine, o_mine, acc, top, pages_out, pages_mid,
    kv_ss, kv_rs, q_ss, q_rs, o_ss, o_rs, z_ss, z_rs, x_ss, x_rs,
    mid_ss, mid_rs, far_ss, far_rs, local_sem,
):
    tokens = q_ref.shape[0]
    rows = groups * tokens
    heads = q_ref.shape[1] // (groups * HEAD)
    wide = heads * HEAD
    half = rows // 2
    span = 2 * zs
    hop = zs // 2
    seq, rep = lax.axis_index("seq"), lax.axis_index("rep")
    z, g = seq // groups, lax.rem(seq, groups)
    x, z_hi = rep // 2, lax.rem(rep, 2)
    z_abs = z_hi * zs + z

    def peer(d):
        return (z * groups + d, rep)

    def along_z(shift, x_at):
        to = lax.rem(z_abs + shift + span, span)
        return (lax.rem(to, zs) * groups + g, x_at * 2 + to // zs)

    def remote(src, dst, ss, rs, device):
        return pltpu.make_async_remote_copy(
            src_ref=src, dst_ref=dst, send_sem=ss, recv_sem=rs,
            device_id=device, device_id_type=MESH,
        )

    barrier = pltpu.get_barrier_semaphore()

    def greet(device):
        pl.semaphore_signal(barrier, inc=1, device_id=device, device_id_type=MESH)

    for i in range(1, groups):
        greet(peer(lax.rem(g + i, groups)))
    for i in range(1, xs):
        greet((seq, lax.rem(x + i, xs) * 2 + z_hi))
    for i in range(xs):
        greet(along_z(hop, i))

    @pl.when(z > 0)
    def _():
        greet((seq - groups, rep))

    cosine, sine = cos_ref[...], sin_ref[...]

    def rotate(head):
        head = head.astype(jnp.float32)
        return (head * cosine + pltpu.roll(head, HEAD // 2, axis=1) * sine).astype(jnp.bfloat16)

    for d in range(groups):
        kv_out[d, :, 0:HEAD] = rotate(k_ref[:, d * HEAD:(d + 1) * HEAD])
        kv_out[d, :, HEAD:2 * HEAD] = v_ref[:, d * HEAD:(d + 1) * HEAD]
    my_rows = pl.ds(pl.multiple_of(g * tokens, tokens), tokens)
    kv_all[z, my_rows, :] = kv_out[g]

    partners = (groups - 1) + (xs - 1) + xs
    pl.semaphore_wait(barrier, partners + jnp.where(z < zs - 1, 1, 0))

    def kv_copy(d, row_of):
        return remote(
            kv_out.at[d],
            kv_all.at[z, pl.ds(pl.multiple_of(row_of * tokens, tokens), tokens)],
            kv_ss.at[d], kv_rs.at[row_of], peer(d),
        )

    for i in range(1, groups):
        kv_copy(lax.rem(g + i, groups), g).start()

    length = len_ref[0]
    owners = [table_ref[j] for j in range(tokens // PAGE)]
    lane = lax.broadcasted_iota(jnp.int32, (1, tokens), 1)
    target = jnp.full((1, tokens), -1, jnp.int32)
    for j, owner in enumerate(owners):
        earlier = jnp.int32(0)
        for i in range(j):
            earlier = earlier + jnp.where(owners[i] == owner, 1, 0)
        owner_x = owner >> 1
        other = jnp.where((owner & 1) == z_hi, 0, xs)
        base = (other + owner_x) * SLOT_ROWS + earlier * PAGE - j * PAGE
        target = jnp.where(
            (lane >= j * PAGE) & (lane < (j + 1) * PAGE) & (earlier < SLOTS), lane + base, target
        )
    target = jnp.where(seq * tokens + lane < length, target, -1)
    slot = lax.broadcasted_iota(jnp.int32, (2 * xs * SLOT_ROWS, tokens), 0)
    chosen = jnp.where(slot == target, 1.0, 0.0).astype(jnp.bfloat16)
    for d in range(groups):
        for part in range(2):
            column = (part * groups + d) * HEAD
            pages_out[:, column:column + HEAD] = jnp.dot(
                chosen, kv_out[d, :, part * HEAD:(part + 1) * HEAD],
                preferred_element_type=jnp.float32,
            ).astype(jnp.bfloat16)

    def slot_rows(i):
        return pl.ds(pl.multiple_of(i * SLOT_ROWS, SLOT_ROWS), SLOT_ROWS)

    def mid_copy(i):
        return remote(
            pages_out.at[slot_rows(xs + i)], pages_mid.at[slot_rows(i)],
            mid_ss.at[i], mid_rs.at[i], along_z(-hop, x),
        )

    def far_copy(i, x_from):
        origin = lax.rem(z_abs + hop, span)
        return remote(
            pages_mid.at[slot_rows(i)], pages_ref.at[slot_rows(x_from * 2 + origin // zs)],
            far_ss.at[i], far_rs.at[x_from], along_z(-hop, i),
        )

    def x_copy(i, x_from):
        return remote(
            pages_out.at[slot_rows(i)], pages_ref.at[slot_rows(x_from * 2 + z_hi)],
            x_ss.at[i], x_rs.at[x_from], (seq, i * 2 + z_hi),
        )

    for i in range(xs):
        mid_copy(i).start()
    for i in range(1, xs):
        x_copy(lax.rem(x + i, xs), x).start()
    own_pages = pltpu.make_async_copy(
        pages_out.at[slot_rows(x)], pages_ref.at[slot_rows(rep)], local_sem.at[0]
    )
    own_pages.start()

    def rotate_queries(d):
        first = d * wide
        for j in range(heads):
            columns = pl.ds(pl.multiple_of(first + j * HEAD, HEAD), HEAD)
            q_out[d, :, j * HEAD:(j + 1) * HEAD] = rotate(q_ref[:, columns])

    def q_copy(d, row_of):
        return remote(
            q_out.at[d], q_mine.at[pl.ds(pl.multiple_of(row_of * tokens, tokens), tokens)],
            q_ss.at[d], q_rs.at[row_of], peer(d),
        )

    def send_queries(i, carry):
        d = lax.rem(g + i, groups)
        rotate_queries(d)
        q_copy(d, g).start()
        return carry

    lax.fori_loop(1, groups, send_queries, 0)
    rotate_queries(g)
    q_mine[my_rows, :] = q_out[g]

    def z_copy(block, part):
        part_rows = kv_all.at[block, pl.ds(part * half, half)]
        at = block * 2 + part
        return remote(part_rows, part_rows, z_ss.at[at], z_rs.at[at], (seq + groups, rep))

    for i in range(1, groups):
        d = lax.rem(g + i, groups)
        kv_copy(d, d).wait_recv()

    @pl.when(z < zs - 1)
    def _():
        for part in range(2):
            z_copy(z, part).start()

    for i in range(1, groups):
        d = lax.rem(g + i, groups)
        q_copy(d, d).wait_recv()

    def attend(block, diagonal):
        chunk = half
        for j in range(heads):
            for c in range(2):
                at = pl.ds(c * chunk, chunk)
                seen = (c + 1) * chunk if diagonal else rows
                keys = kv_all[block, 0:seen, 0:HEAD]
                values = kv_all[block, 0:seen, HEAD:2 * HEAD]
                scores = lax.dot_general(
                    q_mine[at, j * HEAD:(j + 1) * HEAD], keys, NT,
                    preferred_element_type=jnp.float32,
                )
                if diagonal:
                    query_at = lax.broadcasted_iota(jnp.int32, (chunk, seen), 0) + c * chunk
                    key_at = lax.broadcasted_iota(jnp.int32, (chunk, seen), 1)
                    scores = jnp.where(key_at <= query_at, scores, -1e30)
                largest = jnp.max(scores, axis=1, keepdims=True)
                if diagonal:
                    largest = jnp.broadcast_to(largest, (chunk, HEAD))
                else:
                    before = top[j, at, :]
                    largest = jnp.maximum(before, largest)
                    shrink = jnp.exp2((before - largest) * SCALE)
                top[j, at, :] = largest
                shift = jnp.concatenate([largest * SCALE] * max(1, seen // HEAD), axis=1)[:, :seen]
                weights = jnp.exp2(scores * SCALE - shift).astype(jnp.bfloat16)
                extended = jnp.concatenate([values, jnp.ones((seen, HEAD), jnp.bfloat16)], axis=1)
                result = jnp.dot(weights, extended, preferred_element_type=jnp.float32)
                if not diagonal:
                    result = acc[j, at, :] * jnp.concatenate([shrink, shrink], axis=1) + result
                acc[j, at, :] = result

    attend(z, True)

    def step(t, carry):
        @pl.when(t <= z)
        def _():
            block = z - t
            for part in range(2):
                z_copy(block, part).wait_recv()

                @pl.when(z < zs - 1)
                def _():
                    z_copy(block, part).start()
            attend(block, False)

        @pl.when(t <= xs)
        def _():
            mid_copy(t - 1).wait_recv()
            far_copy(t - 1, x).start()
        return carry

    lax.fori_loop(1, max(zs, xs + 1), step, 0)

    def o_copy(d, group_of):
        return remote(
            o_mine.at[pl.ds(pl.multiple_of(d * tokens, tokens), tokens)],
            o_ref.at[:, pl.ds(pl.multiple_of(group_of * wide, wide), wide)],
            o_ss.at[d], o_rs.at[group_of], peer(d),
        )

    def finish(d):
        at = pl.ds(pl.multiple_of(d * tokens, tokens), tokens)
        token = (z * groups + d) * tokens + lax.broadcasted_iota(jnp.int32, (tokens, HEAD), 0)
        for j in range(heads):
            total = acc[j, at, :]
            result = total[:, 0:HEAD] / total[:, HEAD:2 * HEAD]
            o_mine[at, j * HEAD:(j + 1) * HEAD] = jnp.where(token < length, result, 0.0).astype(
                jnp.bfloat16
            )

    def return_rows(i, carry):
        d = lax.rem(g + i, groups)
        finish(d)
        o_copy(d, g).start()
        return carry

    lax.fori_loop(1, groups, return_rows, 0)
    finish(g)
    own_rows = pltpu.make_async_copy(
        o_mine.at[my_rows], o_ref.at[:, pl.ds(pl.multiple_of(g * wide, wide), wide)],
        local_sem.at[1],
    )
    own_rows.start()

    for i in range(1, groups):
        d = lax.rem(g + i, groups)
        kv_copy(d, g).wait_send()
        q_copy(d, g).wait_send()
    for i in range(1, xs):
        other = lax.rem(x + i, xs)
        x_copy(other, x).wait_send()
        x_copy(other, other).wait_recv()
    for i in range(xs):
        mid_copy(i).wait_send()

    @pl.when(z < zs - 1)
    def _():
        def sent(block, carry):
            for part in range(2):
                z_copy(block, part).wait_send()
            return carry

        lax.fori_loop(0, z + 1, sent, 0)

    own_pages.wait()
    own_rows.wait()
    for i in range(1, groups):
        d = lax.rem(g + i, groups)
        o_copy(d, g).wait_send()
        o_copy(d, d).wait_recv()
    for i in range(xs):
        far_copy(i, x).wait_send()
        far_copy(i, i).wait_recv()


def body(query_rows, unrotated_keys, value_projections, lengths, page_table):
    tokens, query_width = query_rows.shape[1:]
    groups = unrotated_keys.shape[2] // HEAD
    zs = lax.axis_size("seq") // groups
    owners = lax.axis_size("rep")
    xs = owners // Z_HALVES
    rows, wide = groups * tokens, query_width // groups
    heads = wide // HEAD
    positions = lax.axis_index("seq") * tokens + jnp.arange(tokens, dtype=jnp.int32)
    cosine, sine = rotary_tables(positions)
    bf16, f32 = jnp.bfloat16, jnp.float32
    vmem = pl.BlockSpec(memory_space=pltpu.VMEM)
    smem = pl.BlockSpec(memory_space=pltpu.SMEM)
    dma = pltpu.SemaphoreType.DMA
    attended, pages = pl.pallas_call(
        functools.partial(kernel, groups, zs, xs),
        out_shape=(
            jax.ShapeDtypeStruct((tokens, query_width), bf16),
            jax.ShapeDtypeStruct((owners * SLOT_ROWS, 2 * groups * HEAD), bf16),
        ),
        in_specs=[vmem] * 5 + [smem] * 2,
        out_specs=(pl.BlockSpec(memory_space=pl.ANY),) * 2,
        scratch_shapes=[
            pltpu.VMEM((groups, tokens, 2 * HEAD), bf16),
            pltpu.VMEM((zs, rows, 2 * HEAD), bf16),
            pltpu.VMEM((groups, tokens, wide), bf16),
            pltpu.VMEM((rows, wide), bf16),
            pltpu.VMEM((rows, wide), bf16),
            pltpu.VMEM((heads, rows, 2 * HEAD), f32),
            pltpu.VMEM((heads, rows, HEAD), f32),
            pltpu.VMEM((owners * SLOT_ROWS, 2 * groups * HEAD), bf16),
            pltpu.VMEM((xs * SLOT_ROWS, 2 * groups * HEAD), bf16),
            dma((groups,)), dma((groups,)), dma((groups,)), dma((groups,)),
            dma((groups,)), dma((groups,)), dma((2 * zs,)), dma((2 * zs,)),
            dma((xs,)), dma((xs,)), dma((xs,)), dma((xs,)), dma((xs,)), dma((xs,)),
            dma((2,)),
        ],
        compiler_params=pltpu.CompilerParams(
            collective_id=0, has_side_effects=True, vmem_limit_bytes=48 * 2**20
        ),
        name="recompute",
    )(
        query_rows[0], unrotated_keys[0], value_projections[0], cosine, sine, lengths,
        page_table[0, :, 0],
    )
    return (
        attended[None],
        pages.reshape(1, 1, owners, SLOTS, PAGE, 2 * groups * HEAD),
    )


def solution(mesh):
    return jax.shard_map(
        body,
        mesh=mesh,
        in_specs=(
            P("rep", "seq", None),
            P("rep", "seq", None),
            P("rep", "seq", None),
            P("rep"),
            P("rep", "seq", None),
        ),
        out_specs=(P("rep", "seq", None), P("rep", "seq", None, None, None, None)),
        check_vma=False,
    )
```

```python
import functools
import math

import jax
import jax.numpy as jnp
from jax import lax
from jax.experimental import pallas as pl
from jax.experimental.pallas import tpu as pltpu
from jax.sharding import PartitionSpec as P

HEAD = 128
PAGE = 8
SLOTS = 2
LEAD = 4
CATCH_UP = (8, 14, 20)
PAGE_STEPS = (7, 13, 18, 23)
SLOT_ROWS = SLOTS * PAGE
Z_HALVES = 2
SCALE = math.log2(math.e) / math.sqrt(HEAD)
MESH = pl.DeviceIdType.MESH
NT = (((1,), (1,)), ((), ()))


def rotary_tables(token_positions):
    halfwidth = HEAD // 2
    frequency = jnp.exp(
        -jnp.arange(halfwidth, dtype=jnp.float32) * (2.0 * math.log(500000.0) / HEAD)
    )
    angles = token_positions.astype(jnp.float32)[:, None] * frequency[None, :]
    cosine, sine = jnp.cos(angles), jnp.sin(angles)
    return (
        jnp.concatenate([cosine, cosine], axis=-1),
        jnp.concatenate([-sine, sine], axis=-1),
    )


def kernel(
    groups, zs, xs,
    q_ref, k_ref, v_ref, cos_ref, sin_ref, len_ref, table_ref,
    o_ref, pages_ref,
    kv_out, kv_all, q_out, q_mine, o_mine, acc, top, pages_out, pages_mid,
    kv_ss, kv_rs, q_ss, q_rs, o_ss, o_rs, z_ss, z_rs, sib_ss, sib_rs, x_ss, x_rs,
    mid_ss, mid_rs, far_ss, far_rs, local_sem,
):
    tokens = q_ref.shape[0]
    rows = groups * tokens
    heads = q_ref.shape[1] // (2 * groups * HEAD)
    wide = heads * HEAD
    half = rows // 2
    quarter = rows // 4
    quarter_shards = groups // 4
    ys = groups // 2
    span = 2 * zs
    hop = zs // 2
    seq, rep = lax.axis_index("seq"), lax.axis_index("rep")
    z, g = seq // groups, lax.rem(seq, groups)
    y, core = g // 2, lax.rem(g, 2)
    my_core = lax.rem(g // quarter_shards, 2)
    x, z_hi = rep // 2, lax.rem(rep, 2)
    z_abs = z_hi * zs + z
    units = z + 1

    def peer(d):
        return (z * groups + d, rep)

    def along_z(shift, x_at):
        to = lax.rem(z_abs + shift + span, span)
        return (lax.rem(to, zs) * groups + g, x_at * 2 + to // zs)

    def remote(src, dst, ss, rs, device):
        return pltpu.make_async_remote_copy(
            src_ref=src, dst_ref=dst, send_sem=ss, recv_sem=rs,
            device_id=device, device_id_type=MESH,
        )

    def token_rows(d):
        return pl.ds(pl.multiple_of(d * tokens, tokens), tokens)

    barrier = pltpu.get_barrier_semaphore()

    def greet(device):
        pl.semaphore_signal(barrier, inc=1, device_id=device, device_id_type=MESH)

    for i in range(1, groups):
        greet(peer(lax.rem(g + i, groups)))
    for i in range(1, xs):
        greet((seq, lax.rem(x + i, xs) * 2 + z_hi))
    for i in range(xs):
        greet(along_z(hop, i))

    @pl.when(z > 0)
    def _():
        greet((seq - groups, rep))

    cosine, sine = cos_ref[...], sin_ref[...]

    def rotate(head):
        head = head.astype(jnp.float32)
        return (head * cosine + pltpu.roll(head, HEAD // 2, axis=1) * sine).astype(jnp.bfloat16)

    for d in range(groups):
        kv_out[d, :, 0:HEAD] = rotate(k_ref[:, d * HEAD:(d + 1) * HEAD])
        kv_out[d, :, HEAD:2 * HEAD] = v_ref[:, d * HEAD:(d + 1) * HEAD]

    @pl.when(my_core == core)
    def _():
        for p in range(2):
            kv_all[p, z, token_rows(g), :] = kv_out[2 * y + p]

    length = len_ref[0]
    owners = [table_ref[j] for j in range(tokens // PAGE)]
    lane = lax.broadcasted_iota(jnp.int32, (1, tokens), 1)
    target = jnp.full((1, tokens), -1, jnp.int32)
    for j, owner in enumerate(owners):
        earlier = jnp.int32(0)
        for i in range(j):
            earlier = earlier + jnp.where(owners[i] == owner, 1, 0)
        owner_x = owner >> 1
        other = jnp.where((owner & 1) == z_hi, 0, xs)
        base = (other + owner_x) * SLOT_ROWS + earlier * PAGE - j * PAGE
        target = jnp.where(
            (lane >= j * PAGE) & (lane < (j + 1) * PAGE) & (earlier < SLOTS), lane + base, target
        )
    target = jnp.where(seq * tokens + lane < length, target, -1)
    slot = lax.broadcasted_iota(jnp.int32, (2 * xs * SLOT_ROWS, tokens), 0)
    chosen = jnp.where(slot == target, 1.0, 0.0).astype(jnp.bfloat16)
    for d in range(groups):
        for part in range(2):
            column = (part * groups + d) * HEAD
            pages_out[:, column:column + HEAD] = jnp.dot(
                chosen, kv_out[d, :, part * HEAD:(part + 1) * HEAD],
                preferred_element_type=jnp.float32,
            ).astype(jnp.bfloat16)

    def rotate_queries(p, d):
        first = ((d // 2 * 2 + p) * 2 + lax.rem(d, 2)) * wide
        for j in range(heads):
            columns = pl.ds(pl.multiple_of(first + j * HEAD, HEAD), HEAD)
            q_out[p, d, :, j * HEAD:(j + 1) * HEAD] = rotate(q_ref[:, columns])

    for p in range(2):
        def one(d, carry):
            rotate_queries(p, d)
            return carry

        lax.fori_loop(0, groups, one, 0)
        q_mine[p, token_rows(g), :] = q_out[p, g]

    partners = (groups - 1) + (xs - 1) + xs
    pl.semaphore_wait(barrier, partners + jnp.where(z < zs - 1, 1, 0))

    def kv_copy(p, y_to, row_of):
        return remote(
            kv_out.at[2 * y_to + p], kv_all.at[p, z, token_rows(row_of)],
            kv_ss.at[p * ys + y_to], kv_rs.at[p * groups + row_of],
            peer(2 * y_to + lax.rem(row_of // quarter_shards, 2)),
        )

    def each_kv_send(act):
        for p in range(2):
            for i in range(1, ys):
                act(kv_copy(p, lax.rem(y + i, ys), g))

            @pl.when(my_core != core)
            def _():
                act(kv_copy(p, y, g))

    each_kv_send(lambda copy: copy.start())

    def place(n):
        late = n >= 3 * units
        t = jnp.where(late, n - 3 * units, n // 3)
        kind = jnp.where(late, 3, n - 3 * t)
        return kind // 2, z - t, lax.rem(kind, 2)

    def quarter_of(p, block, piece, part):
        first = (piece * 2 + part) * quarter
        return kv_all.at[p, block, pl.ds(pl.multiple_of(first, quarter), quarter)]

    def z_copy(p, block, piece):
        at = (p * zs + block) * 2 + piece
        view = quarter_of(p, block, piece, core)
        return remote(view, view, z_ss.at[at], z_rs.at[at], (seq + groups, rep))

    def sib_copy(p, block, piece, part):
        at = (p * zs + block) * 2 + piece
        view = quarter_of(p, block, piece, part)
        return remote(view, view, sib_ss.at[at], sib_rs.at[at], peer(2 * y + 1 - core))

    def forward(n):
        p, block, piece = place(n)

        @pl.when(block == z)
        def _():
            for i in range(quarter_shards):
                source = (piece * 2 + core) * quarter_shards + i

                @pl.when(source != g)
                def _():
                    kv_copy(p, y, source).wait_recv()

        @pl.when(block != z)
        def _():
            z_copy(p, block, piece).wait_recv()

        @pl.when(z < zs - 1)
        def _():
            z_copy(p, block, piece).start()

        sib_copy(p, block, piece, core).start()

    def q_copy(p, d, row_of):
        return remote(
            q_out.at[p, d], q_mine.at[p, token_rows(row_of)],
            q_ss.at[p * groups + d], q_rs.at[p * groups + row_of], peer(d),
        )


    def slot_rows(i):
        return pl.ds(pl.multiple_of(i * SLOT_ROWS, SLOT_ROWS), SLOT_ROWS)

    def mid_copy(i):
        return remote(
            pages_out.at[slot_rows(xs + i)], pages_mid.at[slot_rows(i)],
            mid_ss.at[i], mid_rs.at[i], along_z(-hop, x),
        )

    def far_copy(i, x_from):
        origin = lax.rem(z_abs + hop, span)
        return remote(
            pages_mid.at[slot_rows(i)], pages_ref.at[slot_rows(x_from * 2 + origin // zs)],
            far_ss.at[i], far_rs.at[x_from], along_z(-hop, i),
        )

    def x_copy(i, x_from):
        return remote(
            pages_out.at[slot_rows(i)], pages_ref.at[slot_rows(x_from * 2 + z_hi)],
            x_ss.at[i], x_rs.at[x_from], (seq, i * 2 + z_hi),
        )

    def pass_pages(i):
        mid_copy(i).wait_recv()
        far_copy(i, x).start()

    for i in range(xs):
        mid_copy(i).start()
    for i in range(1, groups):
        q_copy(0, lax.rem(g + i, groups), g).start()
    forward(0)
    for i in range(1, xs):
        x_copy(lax.rem(x + i, xs), x).start()
    own_pages = pltpu.make_async_copy(
        pages_out.at[slot_rows(x)], pages_ref.at[slot_rows(rep)], local_sem.at[0]
    )
    own_pages.start()
    forward(1)
    for i in range(1, groups):
        q_copy(1, lax.rem(g + i, groups), g).start()
    for n in range(2, 4):
        forward(n)

    @pl.when(units > 1)
    def _():
        forward(4)

    def attend(p, block, piece, chunks, diagonal, first):
        keys_at = pl.ds(piece * half, half) if isinstance(piece, int) else pl.ds(
            pl.multiple_of(piece * half, half), half
        )
        keys = kv_all[p, block, keys_at, 0:HEAD]
        values = kv_all[p, block, keys_at, HEAD:2 * HEAD]
        extended = jnp.concatenate([values, jnp.ones((half, HEAD), jnp.bfloat16)], axis=1)
        for j in range(heads):
            for c in chunks:
                at = pl.ds(c * half, half)
                scores = lax.dot_general(
                    q_mine[p, at, j * HEAD:(j + 1) * HEAD], keys, NT,
                    preferred_element_type=jnp.float32,
                )
                if c == diagonal:
                    query_at = lax.broadcasted_iota(jnp.int32, (half, half), 0)
                    key_at = lax.broadcasted_iota(jnp.int32, (half, half), 1)
                    scores = jnp.where(key_at <= query_at, scores, -1e30)
                largest = jnp.max(scores, axis=1, keepdims=True)
                if first:
                    largest = jnp.broadcast_to(largest, (half, HEAD))
                else:
                    before = top[p, j, at, :]
                    largest = jnp.maximum(before, largest)
                    shrink = jnp.exp2((before - largest) * SCALE)
                top[p, j, at, :] = largest
                shift = jnp.concatenate([largest * SCALE] * max(1, half // HEAD), axis=1)[:, :half]
                weights = jnp.exp2(scores * SCALE - shift).astype(jnp.bfloat16)
                result = jnp.dot(weights, extended, preferred_element_type=jnp.float32)
                if not first:
                    result = acc[p, j, at, :] * jnp.concatenate([shrink, shrink], axis=1) + result
                acc[p, j, at, :] = result

    def o_columns(p, d):
        first = ((d // 2 * 2 + p) * 2 + lax.rem(d, 2)) * wide
        return o_ref.at[:, pl.ds(pl.multiple_of(first, wide), wide)]

    def o_copy(p, d, group_of):
        return remote(
            o_mine.at[p, token_rows(d)], o_columns(p, group_of),
            o_ss.at[p * groups + d], o_rs.at[p * groups + group_of], peer(d),
        )

    def own_rows(p):
        return pltpu.make_async_copy(
            o_mine.at[p, token_rows(g)], o_columns(p, g), local_sem.at[1 + p]
        )

    def finish(p, d):
        token = (z * groups + d) * tokens + lax.broadcasted_iota(jnp.int32, (tokens, HEAD), 0)
        for j in range(heads):
            total = acc[p, j, token_rows(d), :]
            result = total[:, 0:HEAD] / total[:, HEAD:2 * HEAD]
            o_mine[p, token_rows(d), j * HEAD:(j + 1) * HEAD] = jnp.where(
                token < length, result, 0.0
            ).astype(jnp.bfloat16)

    def step(i, carry):
        ahead = i + LEAD
        fresh = i >= 1
        for at in CATCH_UP:
            ahead = ahead - jnp.where(i >= at, 1, 0)
            fresh = fresh & (i != at)

        @pl.when(fresh & (ahead < 4 * units))
        def _():
            forward(ahead)

        moved = jnp.where(i == 4, 2, jnp.where((i == 2) | (i == 3), i + 1, i))
        n = jnp.where(units > 1, moved, i)
        p, block, piece = place(n)
        sib_copy(p, block, piece, 1 - core).wait_recv()

        @pl.when((block == z) & (piece == 0))
        def _():
            for d in range(1, groups):
                source = lax.rem(g + d, groups)
                q_copy(p, source, source).wait_recv()
            attend(p, block, 0, (0, 1), 0, True)

        @pl.when((block == z) & (piece == 1))
        def _():
            attend(p, block, 1, (1,), 1, False)

        @pl.when(block != z)
        def _():
            attend(p, block, piece, (0, 1), None, False)

        @pl.when((block == 0) & (piece == 1))
        def _():
            def return_rows(i, carry):
                d = lax.rem(g + i, groups)
                finish(p, d)
                o_copy(p, d, g).start()
                return carry

            lax.fori_loop(1, groups, return_rows, 0)
            finish(p, g)
            own_rows(p).start()

        for part in range(xs):
            @pl.when(i == PAGE_STEPS[part])
            def _():
                pass_pages(part)

        return carry

    lax.fori_loop(0, 4 * units, step, 0)

    for i in range(xs):
        @pl.when(PAGE_STEPS[i] >= 4 * units)
        def _():
            pass_pages(i)

    each_kv_send(lambda copy: copy.wait_send())
    for p in range(2):
        for i in range(1, groups):
            q_copy(p, lax.rem(g + i, groups), g).wait_send()
    for i in range(1, xs):
        other = lax.rem(x + i, xs)
        x_copy(other, x).wait_send()
        x_copy(other, other).wait_recv()
    for i in range(xs):
        mid_copy(i).wait_send()

    def sent(n, carry):
        p, block, piece = place(n)
        sib_copy(p, block, piece, core).wait_send()

        @pl.when(z < zs - 1)
        def _():
            z_copy(p, block, piece).wait_send()

        return carry

    lax.fori_loop(0, 4 * units, sent, 0)
    own_pages.wait()
    for p in range(2):
        own_rows(p).wait()
        for i in range(1, groups):
            d = lax.rem(g + i, groups)
            o_copy(p, d, g).wait_send()
            o_copy(p, d, d).wait_recv()
    for i in range(xs):
        far_copy(i, x).wait_send()
        far_copy(i, i).wait_recv()


def body(query_rows, unrotated_keys, value_projections, lengths, page_table):
    tokens, query_width = query_rows.shape[1:]
    groups = unrotated_keys.shape[2] // HEAD
    zs = lax.axis_size("seq") // groups
    owners = lax.axis_size("rep")
    xs = owners // Z_HALVES
    rows, wide = groups * tokens, query_width // (2 * groups)
    heads = wide // HEAD
    positions = lax.axis_index("seq") * tokens + jnp.arange(tokens, dtype=jnp.int32)
    cosine, sine = rotary_tables(positions)
    bf16, f32 = jnp.bfloat16, jnp.float32
    vmem = pl.BlockSpec(memory_space=pltpu.VMEM)
    smem = pl.BlockSpec(memory_space=pltpu.SMEM)
    dma = pltpu.SemaphoreType.DMA
    attended, pages = pl.pallas_call(
        functools.partial(kernel, groups, zs, xs),
        out_shape=(
            jax.ShapeDtypeStruct((tokens, query_width), bf16),
            jax.ShapeDtypeStruct((owners * SLOT_ROWS, 2 * groups * HEAD), bf16),
        ),
        in_specs=[vmem] * 5 + [smem] * 2,
        out_specs=(pl.BlockSpec(memory_space=pl.ANY),) * 2,
        scratch_shapes=[
            pltpu.VMEM((groups, tokens, 2 * HEAD), bf16),
            pltpu.VMEM((2, zs, rows, 2 * HEAD), bf16),
            pltpu.VMEM((2, groups, tokens, wide), bf16),
            pltpu.VMEM((2, rows, wide), bf16),
            pltpu.VMEM((2, rows, wide), bf16),
            pltpu.VMEM((2, heads, rows, 2 * HEAD), f32),
            pltpu.VMEM((2, heads, rows, HEAD), f32),
            pltpu.VMEM((owners * SLOT_ROWS, 2 * groups * HEAD), bf16),
            pltpu.VMEM((xs * SLOT_ROWS, 2 * groups * HEAD), bf16),
            dma((groups,)), dma((2 * groups,)), dma((2 * groups,)), dma((2 * groups,)),
            dma((2 * groups,)), dma((2 * groups,)), dma((4 * zs,)), dma((4 * zs,)),
            dma((4 * zs,)), dma((4 * zs,)),
            dma((xs,)), dma((xs,)), dma((xs,)), dma((xs,)), dma((xs,)), dma((xs,)),
            dma((3,)),
        ],
        compiler_params=pltpu.CompilerParams(
            collective_id=0, has_side_effects=True, vmem_limit_bytes=48 * 2**20
        ),
        name="recompute",
    )(
        query_rows[0], unrotated_keys[0], value_projections[0], cosine, sine, lengths,
        page_table[0, :, 0],
    )
    return (
        attended[None],
        pages.reshape(1, 1, owners, SLOTS, PAGE, 2 * groups * HEAD),
    )


def solution(mesh):
    return jax.shard_map(
        body,
        mesh=mesh,
        in_specs=(
            P("rep", "seq", None),
            P("rep", "seq", None),
            P("rep", "seq", None),
            P("rep"),
            P("rep", "seq", None),
        ),
        out_specs=(P("rep", "seq", None), P("rep", "seq", None, None, None, None)),
        check_vma=False,
    )
```

```python
import functools
import math

import jax
import jax.numpy as jnp
from jax import lax
from jax.experimental import pallas as pl
from jax.experimental.pallas import tpu as pltpu
from jax.sharding import PartitionSpec as P

HEAD = 128
PAGE = 8
SLOTS = 2
LEAD = 6
CATCH_UP = (5, 9, 13, 17, 21)
ORDER_TWO = (0, 1, 3, 4, 2, 5)
ORDER_MORE = (0, 1, 3, 4, 6, 7, 2, 5, 8)
PAGE_STEPS = (6, 11, 15, 19)
SLOT_ROWS = SLOTS * PAGE
Z_HALVES = 2
SCALE = math.log2(math.e) / math.sqrt(HEAD)
MESH = pl.DeviceIdType.MESH
NT = (((1,), (1,)), ((), ()))


def both_ways(n):
    first = [2, n - 2, 3, n - 1, n // 2, n // 2 + 1]
    return list(dict.fromkeys([i for i in first if 1 < i < n] + list(range(n - 1, 0, -1))))


def wrap(value, n):
    return jnp.where(value >= n, value - n, value)


def rotary_tables(token_positions):
    halfwidth = HEAD // 2
    frequency = jnp.exp(
        -jnp.arange(halfwidth, dtype=jnp.float32) * (2.0 * math.log(500000.0) / HEAD)
    )
    angles = token_positions.astype(jnp.float32)[:, None] * frequency[None, :]
    cosine, sine = jnp.cos(angles), jnp.sin(angles)
    return (
        jnp.concatenate([cosine, cosine], axis=-1),
        jnp.concatenate([-sine, sine], axis=-1),
    )


def kernel(
    groups, zs, xs,
    q_ref, k_ref, v_ref, cos_ref, sin_ref, len_ref, table_ref,
    o_ref, pages_ref,
    kv_out, kv_all, q_out, q_mine, o_mine, acc, top, pages_out, pages_mid,
    kv_ss, kv_rs, q_ss, q_rs, o_ss, o_rs, z_ss, z_rs, sib_ss, sib_rs, x_ss, x_rs,
    mid_ss, mid_rs, far_ss, far_rs, local_sem,
):
    tokens = q_ref.shape[0]
    rows = groups * tokens
    heads = q_ref.shape[1] // (2 * groups * HEAD)
    wide = heads * HEAD
    half = rows // 2
    quarter = rows // 4
    quarter_shards = groups // 4
    ys = groups // 2
    hop = zs // 2
    seq, rep = lax.axis_index("seq"), lax.axis_index("rep")
    z, g = seq // groups, lax.rem(seq, groups)
    y, core = g // 2, lax.rem(g, 2)
    my_core = lax.rem(g // quarter_shards, 2)
    x, z_hi = rep // 2, lax.rem(rep, 2)
    units = z + 1

    def peer(d):
        return (z * groups + d, rep)

    def along_z(shift, x_at):
        inside = (z + shift >= 0) & (z + shift < zs)
        step = jnp.where(inside, shift, jnp.where(z + shift < 0, shift + zs, shift - zs))
        return (seq + step * groups, x_at * 2 + jnp.where(inside, z_hi, 1 - z_hi))

    def remote(src, dst, ss, rs, device):
        return pltpu.make_async_remote_copy(
            src_ref=src, dst_ref=dst, send_sem=ss, recv_sem=rs,
            device_id=device, device_id_type=MESH,
        )

    def token_rows(d):
        return pl.ds(pl.multiple_of(d * tokens, tokens), tokens)

    barrier = pltpu.get_barrier_semaphore()

    def greet(device):
        pl.semaphore_signal(barrier, inc=1, device_id=device, device_id_type=MESH)

    for i in range(1, groups):
        greet(peer(wrap(g + i, groups)))
    for i in range(1, xs):
        greet((seq, wrap(x + i, xs) * 2 + z_hi))
    for i in range(xs):
        greet(along_z(hop, i))

    @pl.when(z > 0)
    def _():
        greet((seq - groups, rep))

    cosine, sine = cos_ref[...], sin_ref[...]

    def rotate(head):
        head = head.astype(jnp.float32)
        return (head * cosine + pltpu.roll(head, HEAD // 2, axis=1) * sine).astype(jnp.bfloat16)

    for d in range(groups):
        kv_out[d, :, 0:HEAD] = rotate(k_ref[:, d * HEAD:(d + 1) * HEAD])
        kv_out[d, :, HEAD:2 * HEAD] = v_ref[:, d * HEAD:(d + 1) * HEAD]

    @pl.when(my_core == core)
    def _():
        for p in range(2):
            kv_all[p, z, token_rows(g), :] = kv_out[2 * y + p]

    length = len_ref[0]
    owners = [table_ref[j] for j in range(tokens // PAGE)]
    lane = lax.broadcasted_iota(jnp.int32, (1, tokens), 1)
    target = jnp.full((1, tokens), -1, jnp.int32)
    for j, owner in enumerate(owners):
        earlier = jnp.int32(0)
        for i in range(j):
            earlier = earlier + jnp.where(owners[i] == owner, 1, 0)
        owner_x = owner >> 1
        other = jnp.where((owner & 1) == z_hi, 0, xs)
        base = (other + owner_x) * SLOT_ROWS + earlier * PAGE - j * PAGE
        target = jnp.where(
            (lane >= j * PAGE) & (lane < (j + 1) * PAGE) & (earlier < SLOTS), lane + base, target
        )
    target = jnp.where(seq * tokens + lane < length, target, -1)
    slot = lax.broadcasted_iota(jnp.int32, (2 * xs * SLOT_ROWS, tokens), 0)
    chosen = jnp.where(slot == target, 1.0, 0.0).astype(jnp.bfloat16)
    for d in range(groups):
        for part in range(2):
            column = (part * groups + d) * HEAD
            pages_out[:, column:column + HEAD] = jnp.dot(
                chosen, kv_out[d, :, part * HEAD:(part + 1) * HEAD],
                preferred_element_type=jnp.float32,
            ).astype(jnp.bfloat16)

    def rotate_queries(p, d):
        first = ((d // 2 * 2 + p) * 2 + lax.rem(d, 2)) * wide
        for j in range(heads):
            columns = pl.ds(pl.multiple_of(first + j * HEAD, HEAD), HEAD)
            q_out[p, d, :, j * HEAD:(j + 1) * HEAD] = rotate(q_ref[:, columns])

    for p in range(2):
        def one(d, carry):
            rotate_queries(p, d)
            return carry

        lax.fori_loop(0, groups, one, 0)
        q_mine[p, token_rows(g), :] = q_out[p, g]

    partners = (groups - 1) + (xs - 1) + xs
    pl.semaphore_wait(barrier, partners + jnp.where(z < zs - 1, 1, 0))

    def kv_copy(p, y_to, row_of):
        return remote(
            kv_out.at[2 * y_to + p], kv_all.at[p, z, token_rows(row_of)],
            kv_ss.at[p * ys + y_to], kv_rs.at[p * groups + row_of],
            peer(2 * y_to + lax.rem(row_of // quarter_shards, 2)),
        )

    def each_kv_send(act):
        for p in range(2):
            for i in sorted(range(1, ys), key=lambda i: abs(i - ys / 2), reverse=True):
                act(kv_copy(p, wrap(y + i, ys), g))

            @pl.when(my_core != core)
            def _():
                act(kv_copy(p, y, g))

    each_kv_send(lambda copy: copy.start())

    def place(n):
        late = n >= 3 * units
        t = jnp.where(late, n - 3 * units, n // 3)
        kind = jnp.where(late, 3, n - 3 * t)
        return kind // 2, z - t, lax.rem(kind, 2)

    def quarter_of(p, block, piece, part):
        first = (piece * 2 + part) * quarter
        return kv_all.at[p, block, pl.ds(pl.multiple_of(first, quarter), quarter)]

    def z_copy(p, block, piece):
        at = (p * zs + block) * 2 + piece
        view = quarter_of(p, block, piece, core)
        return remote(view, view, z_ss.at[at], z_rs.at[at], (seq + groups, rep))

    def sib_copy(p, block, piece, part):
        at = (p * zs + block) * 2 + piece
        view = quarter_of(p, block, piece, part)
        return remote(view, view, sib_ss.at[at], sib_rs.at[at], peer(2 * y + 1 - core))

    def forward(n):
        p, block, piece = place(n)

        @pl.when(block == z)
        def _():
            for i in range(quarter_shards):
                source = (piece * 2 + core) * quarter_shards + i

                @pl.when(source != g)
                def _():
                    kv_copy(p, y, source).wait_recv()

        @pl.when(block != z)
        def _():
            z_copy(p, block, piece).wait_recv()

        @pl.when(z < zs - 1)
        def _():
            z_copy(p, block, piece).start()

        sib_copy(p, block, piece, core).start()

    def q_copy(p, d, row_of):
        return remote(
            q_out.at[p, d], q_mine.at[p, token_rows(row_of)],
            q_ss.at[p * groups + d], q_rs.at[p * groups + row_of], peer(d),
        )


    def slot_rows(i):
        return pl.ds(pl.multiple_of(i * SLOT_ROWS, SLOT_ROWS), SLOT_ROWS)

    def mid_copy(i):
        return remote(
            pages_out.at[slot_rows(xs + i)], pages_mid.at[slot_rows(i)],
            mid_ss.at[i], mid_rs.at[i], along_z(-hop, x),
        )

    def far_copy(i, x_from):
        origin_hi = jnp.where(z + hop < zs, z_hi, 1 - z_hi)
        return remote(
            pages_mid.at[slot_rows(i)], pages_ref.at[slot_rows(x_from * 2 + origin_hi)],
            far_ss.at[i], far_rs.at[x_from], along_z(-hop, i),
        )

    def x_copy(i, x_from):
        return remote(
            pages_out.at[slot_rows(i)], pages_ref.at[slot_rows(x_from * 2 + z_hi)],
            x_ss.at[i], x_rs.at[x_from], (seq, i * 2 + z_hi),
        )

    def pass_pages(i):
        mid_copy(i).wait_recv()
        far_copy(i, x).start()

    for i in range(xs):
        mid_copy(i).start()
    for i in both_ways(groups):
        q_copy(0, wrap(g + i, groups), g).start()
    forward(0)
    for i in range(1, xs):
        x_copy(wrap(x + i, xs), x).start()
    own_pages = pltpu.make_async_copy(
        pages_out.at[slot_rows(x)], pages_ref.at[slot_rows(rep)], local_sem.at[0]
    )
    own_pages.start()
    forward(1)
    for i in both_ways(groups):
        q_copy(1, wrap(g + i, groups), g).start()
    for n in range(2, 4):
        forward(n)

    @pl.when(units > 1)
    def _():
        for n in range(4, LEAD + 1):
            forward(n)

    def attend(p, block, piece, chunks, diagonal, first):
        keys_at = pl.ds(piece * half, half) if isinstance(piece, int) else pl.ds(
            pl.multiple_of(piece * half, half), half
        )
        keys = kv_all[p, block, keys_at, 0:HEAD]
        values = kv_all[p, block, keys_at, HEAD:2 * HEAD]
        extended = jnp.concatenate([values, jnp.ones((half, HEAD), jnp.bfloat16)], axis=1)
        for j in range(heads):
            for c in chunks:
                at = pl.ds(c * half, half)
                scores = lax.dot_general(
                    q_mine[p, at, j * HEAD:(j + 1) * HEAD], keys, NT,
                    preferred_element_type=jnp.float32,
                )
                if c == diagonal:
                    query_at = lax.broadcasted_iota(jnp.int32, (half, half), 0)
                    key_at = lax.broadcasted_iota(jnp.int32, (half, half), 1)
                    scores = jnp.where(key_at <= query_at, scores, -1e30)
                largest = jnp.max(scores, axis=1, keepdims=True)
                if first:
                    largest = jnp.broadcast_to(largest, (half, HEAD))
                else:
                    before = top[p, j, at, :]
                    largest = jnp.maximum(before, largest)
                    shrink = jnp.exp2((before - largest) * SCALE)
                top[p, j, at, :] = largest
                shift = jnp.concatenate([largest * SCALE] * max(1, half // HEAD), axis=1)[:, :half]
                weights = jnp.exp2(scores * SCALE - shift).astype(jnp.bfloat16)
                result = jnp.dot(weights, extended, preferred_element_type=jnp.float32)
                if not first:
                    result = acc[p, j, at, :] * jnp.concatenate([shrink, shrink], axis=1) + result
                acc[p, j, at, :] = result

    def o_columns(p, d):
        first = ((d // 2 * 2 + p) * 2 + lax.rem(d, 2)) * wide
        return o_ref.at[:, pl.ds(pl.multiple_of(first, wide), wide)]

    def o_copy(p, d, group_of):
        return remote(
            o_mine.at[p, token_rows(d)], o_columns(p, group_of),
            o_ss.at[p * groups + d], o_rs.at[p * groups + group_of], peer(d),
        )

    def own_rows(p):
        return pltpu.make_async_copy(
            o_mine.at[p, token_rows(g)], o_columns(p, g), local_sem.at[1 + p]
        )

    def finish(p, d):
        token = (z * groups + d) * tokens + lax.broadcasted_iota(jnp.int32, (tokens, HEAD), 0)
        for j in range(heads):
            total = acc[p, j, token_rows(d), :]
            result = total[:, 0:HEAD] / total[:, HEAD:2 * HEAD]
            o_mine[p, token_rows(d), j * HEAD:(j + 1) * HEAD] = jnp.where(
                token < length, result, 0.0
            ).astype(jnp.bfloat16)

    def step(i, carry):
        ahead = i + LEAD
        fresh = i >= 1
        for at in CATCH_UP:
            ahead = ahead - jnp.where(i >= at, 1, 0)
            fresh = fresh & (i != at)

        @pl.when(fresh & (ahead < 4 * units))
        def _():
            forward(ahead)

        n = i
        for known, order in ((units == 2, ORDER_TWO), (units > 2, ORDER_MORE)):
            for at, index in enumerate(order):
                n = jnp.where(known & (i == at), index, n)
        p, block, piece = place(n)
        sib_copy(p, block, piece, 1 - core).wait_recv()

        @pl.when((block == z) & (piece == 0))
        def _():
            for d in range(1, groups):
                source = wrap(g + d, groups)
                q_copy(p, source, source).wait_recv()
            attend(p, block, 0, (0, 1), 0, True)

        @pl.when((block == z) & (piece == 1))
        def _():
            attend(p, block, 1, (1,), 1, False)

        @pl.when(block != z)
        def _():
            attend(p, block, piece, (0, 1), None, False)

        @pl.when((block == 0) & (piece == 1))
        def _():
            for offset in both_ways(groups):
                d = wrap(g + offset, groups)
                finish(p, d)
                o_copy(p, d, g).start()
            finish(p, g)
            own_rows(p).start()

        for part in range(xs):
            @pl.when(i == PAGE_STEPS[part])
            def _():
                pass_pages(part)

        return carry

    lax.fori_loop(0, 4 * units, step, 0)

    for i in range(xs):
        @pl.when(PAGE_STEPS[i] >= 4 * units)
        def _():
            pass_pages(i)

    each_kv_send(lambda copy: copy.wait_send())
    for p in range(2):
        for i in range(1, groups):
            q_copy(p, wrap(g + i, groups), g).wait_send()
    for i in range(1, xs):
        other = wrap(x + i, xs)
        x_copy(other, x).wait_send()
        x_copy(other, other).wait_recv()
    for i in range(xs):
        mid_copy(i).wait_send()

    def sent(n, carry):
        p, block, piece = place(n)
        sib_copy(p, block, piece, core).wait_send()

        @pl.when(z < zs - 1)
        def _():
            z_copy(p, block, piece).wait_send()

        return carry

    lax.fori_loop(0, 4 * units, sent, 0)
    own_pages.wait()
    for p in range(2):
        own_rows(p).wait()
        for i in range(1, groups):
            d = wrap(g + i, groups)
            o_copy(p, d, g).wait_send()
            o_copy(p, d, d).wait_recv()
    for i in range(xs):
        far_copy(i, x).wait_send()
        far_copy(i, i).wait_recv()


def body(query_rows, unrotated_keys, value_projections, lengths, page_table):
    tokens, query_width = query_rows.shape[1:]
    groups = unrotated_keys.shape[2] // HEAD
    zs = lax.axis_size("seq") // groups
    owners = lax.axis_size("rep")
    xs = owners // Z_HALVES
    rows, wide = groups * tokens, query_width // (2 * groups)
    heads = wide // HEAD
    positions = lax.axis_index("seq") * tokens + jnp.arange(tokens, dtype=jnp.int32)
    cosine, sine = rotary_tables(positions)
    bf16, f32 = jnp.bfloat16, jnp.float32
    vmem = pl.BlockSpec(memory_space=pltpu.VMEM)
    smem = pl.BlockSpec(memory_space=pltpu.SMEM)
    dma = pltpu.SemaphoreType.DMA
    attended, pages = pl.pallas_call(
        functools.partial(kernel, groups, zs, xs),
        out_shape=(
            jax.ShapeDtypeStruct((tokens, query_width), bf16),
            jax.ShapeDtypeStruct((owners * SLOT_ROWS, 2 * groups * HEAD), bf16),
        ),
        in_specs=[vmem] * 5 + [smem] * 2,
        out_specs=(pl.BlockSpec(memory_space=pl.ANY),) * 2,
        scratch_shapes=[
            pltpu.VMEM((groups, tokens, 2 * HEAD), bf16),
            pltpu.VMEM((2, zs, rows, 2 * HEAD), bf16),
            pltpu.VMEM((2, groups, tokens, wide), bf16),
            pltpu.VMEM((2, rows, wide), bf16),
            pltpu.VMEM((2, rows, wide), bf16),
            pltpu.VMEM((2, heads, rows, 2 * HEAD), f32),
            pltpu.VMEM((2, heads, rows, HEAD), f32),
            pltpu.VMEM((owners * SLOT_ROWS, 2 * groups * HEAD), bf16),
            pltpu.VMEM((xs * SLOT_ROWS, 2 * groups * HEAD), bf16),
            dma((groups,)), dma((2 * groups,)), dma((2 * groups,)), dma((2 * groups,)),
            dma((2 * groups,)), dma((2 * groups,)), dma((4 * zs,)), dma((4 * zs,)),
            dma((4 * zs,)), dma((4 * zs,)),
            dma((xs,)), dma((xs,)), dma((xs,)), dma((xs,)), dma((xs,)), dma((xs,)),
            dma((3,)),
        ],
        compiler_params=pltpu.CompilerParams(
            collective_id=0, has_side_effects=True, vmem_limit_bytes=48 * 2**20
        ),
        name="recompute",
    )(
        query_rows[0], unrotated_keys[0], value_projections[0], cosine, sine, lengths,
        page_table[0, :, 0],
    )
    return (
        attended[None],
        pages.reshape(1, 1, owners, SLOTS, PAGE, 2 * groups * HEAD),
    )


def solution(mesh):
    return jax.shard_map(
        body,
        mesh=mesh,
        in_specs=(
            P("rep", "seq", None),
            P("rep", "seq", None),
            P("rep", "seq", None),
            P("rep"),
            P("rep", "seq", None),
        ),
        out_specs=(P("rep", "seq", None), P("rep", "seq", None, None, None, None)),
        check_vma=False,
    )
```

```python
import functools
import math

import jax
import jax.numpy as jnp
from jax import lax
from jax.experimental import pallas as pl
from jax.experimental.pallas import tpu as pltpu
from jax.sharding import PartitionSpec as P

HEAD = 128
PAGE = 8
SLOTS = 2
LEAD = 6
CATCH_UP = (5, 9, 13, 17, 21)
ORDER_TWO = (0, 1, 3, 4, 2, 5)
ORDER_MORE = (0, 1, 3, 4, 6, 7, 2, 5, 8)
PAGE_STEPS = (5, 9, 13, 17)
SLOT_ROWS = SLOTS * PAGE
Z_HALVES = 2
SCALE = math.log2(math.e) / math.sqrt(HEAD)
MESH = pl.DeviceIdType.MESH
NT = (((1,), (1,)), ((), ()))


def both_ways(n):
    first = [2, n - 2, 3, n - 1, n // 2, n // 2 + 1]
    return list(dict.fromkeys([i for i in first if 1 < i < n] + list(range(n - 1, 0, -1))))


def wrap(value, n):
    return jnp.where(value >= n, value - n, value)


def rotary_tables(token_positions):
    halfwidth = HEAD // 2
    frequency = jnp.exp(
        -jnp.arange(halfwidth, dtype=jnp.float32) * (2.0 * math.log(500000.0) / HEAD)
    )
    angles = token_positions.astype(jnp.float32)[:, None] * frequency[None, :]
    cosine, sine = jnp.cos(angles), jnp.sin(angles)
    return (
        jnp.concatenate([cosine, cosine], axis=-1),
        jnp.concatenate([-sine, sine], axis=-1),
    )


def kernel(
    groups, zs, xs,
    q_ref, k_ref, v_ref, cos_ref, sin_ref, len_ref, table_ref,
    o_ref, pages_ref,
    kv_out, kv_all, q_out, q_mine, o_mine, acc, top, pages_out, pages_mid,
    kv_ss, kv_rs, q_ss, q_rs, o_ss, o_rs, z_ss, z_rs, sib_ss, sib_rs, x_ss, x_rs,
    mid_ss, mid_rs, far_ss, far_rs, local_sem,
):
    tokens = q_ref.shape[0]
    rows = groups * tokens
    heads = q_ref.shape[1] // (2 * groups * HEAD)
    wide = heads * HEAD
    half = rows // 2
    quarter = rows // 4
    quarter_shards = groups // 4
    ys = groups // 2
    hop = zs // 2
    seq, rep = lax.axis_index("seq"), lax.axis_index("rep")
    z, g = seq // groups, lax.rem(seq, groups)
    y, core = g // 2, lax.rem(g, 2)
    my_core = lax.rem(g // quarter_shards, 2)
    x, z_hi = rep // 2, lax.rem(rep, 2)
    units = z + 1

    def peer(d):
        return (z * groups + d, rep)

    def along_z(shift, x_at):
        inside = (z + shift >= 0) & (z + shift < zs)
        step = jnp.where(inside, shift, jnp.where(z + shift < 0, shift + zs, shift - zs))
        return (seq + step * groups, x_at * 2 + jnp.where(inside, z_hi, 1 - z_hi))

    def remote(src, dst, ss, rs, device):
        return pltpu.make_async_remote_copy(
            src_ref=src, dst_ref=dst, send_sem=ss, recv_sem=rs,
            device_id=device, device_id_type=MESH,
        )

    def token_rows(d):
        return pl.ds(pl.multiple_of(d * tokens, tokens), tokens)

    barrier = pltpu.get_barrier_semaphore()

    def greet(device):
        pl.semaphore_signal(barrier, inc=1, device_id=device, device_id_type=MESH)

    for i in range(1, groups):
        greet(peer(wrap(g + i, groups)))
    for i in range(1, xs):
        greet((seq, wrap(x + i, xs) * 2 + z_hi))
    for i in range(xs):
        greet(along_z(hop, i))

    @pl.when(z > 0)
    def _():
        greet((seq - groups, rep))

    cosine, sine = cos_ref[...], sin_ref[...]

    def rotate(head):
        head = head.astype(jnp.float32)
        return (head * cosine + pltpu.roll(head, HEAD // 2, axis=1) * sine).astype(jnp.bfloat16)

    for d in range(groups):
        kv_out[d, :, 0:HEAD] = rotate(k_ref[:, d * HEAD:(d + 1) * HEAD])
        kv_out[d, :, HEAD:2 * HEAD] = v_ref[:, d * HEAD:(d + 1) * HEAD]

    @pl.when(my_core == core)
    def _():
        for p in range(2):
            kv_all[p, z, token_rows(g), :] = kv_out[2 * y + p]

    length = len_ref[0]
    owners = [table_ref[j] for j in range(tokens // PAGE)]
    lane = lax.broadcasted_iota(jnp.int32, (1, tokens), 1)
    target = jnp.full((1, tokens), -1, jnp.int32)
    for j, owner in enumerate(owners):
        earlier = jnp.int32(0)
        for i in range(j):
            earlier = earlier + jnp.where(owners[i] == owner, 1, 0)
        owner_x = owner >> 1
        other = jnp.where((owner & 1) == z_hi, 0, xs)
        base = (other + owner_x) * SLOT_ROWS + earlier * PAGE - j * PAGE
        target = jnp.where(
            (lane >= j * PAGE) & (lane < (j + 1) * PAGE) & (earlier < SLOTS), lane + base, target
        )
    target = jnp.where(seq * tokens + lane < length, target, -1)
    slot = lax.broadcasted_iota(jnp.int32, (2 * xs * SLOT_ROWS, tokens), 0)
    chosen = jnp.where(slot == target, 1.0, 0.0).astype(jnp.bfloat16)
    for d in range(groups):
        for part in range(2):
            column = (part * groups + d) * HEAD
            pages_out[:, column:column + HEAD] = jnp.dot(
                chosen, kv_out[d, :, part * HEAD:(part + 1) * HEAD],
                preferred_element_type=jnp.float32,
            ).astype(jnp.bfloat16)

    def rotate_queries(p, d):
        first = ((d // 2 * 2 + p) * 2 + lax.rem(d, 2)) * wide
        for j in range(heads):
            columns = pl.ds(pl.multiple_of(first + j * HEAD, HEAD), HEAD)
            q_out[p, d, :, j * HEAD:(j + 1) * HEAD] = rotate(q_ref[:, columns])

    for p in range(2):
        def one(d, carry):
            rotate_queries(p, d)
            return carry

        lax.fori_loop(0, groups, one, 0)
        q_mine[p, token_rows(g), :] = q_out[p, g]

    partners = (groups - 1) + (xs - 1) + xs
    pl.semaphore_wait(barrier, partners + jnp.where(z < zs - 1, 1, 0))

    def kv_copy(p, y_to, row_of):
        return remote(
            kv_out.at[2 * y_to + p], kv_all.at[p, z, token_rows(row_of)],
            kv_ss.at[p * ys + y_to], kv_rs.at[p * groups + row_of],
            peer(2 * y_to + lax.rem(row_of // quarter_shards, 2)),
        )

    def each_kv_send(act):
        for p in range(2):
            for i in sorted(range(1, ys), key=lambda i: abs(i - ys / 2), reverse=True):
                act(kv_copy(p, wrap(y + i, ys), g))

            @pl.when(my_core != core)
            def _():
                act(kv_copy(p, y, g))

    each_kv_send(lambda copy: copy.start())

    def place(n):
        late = n >= 3 * units
        t = jnp.where(late, n - 3 * units, n // 3)
        kind = jnp.where(late, 3, n - 3 * t)
        return kind // 2, z - t, lax.rem(kind, 2)

    def quarter_of(p, block, piece, part):
        first = (piece * 2 + part) * quarter
        return kv_all.at[p, block, pl.ds(pl.multiple_of(first, quarter), quarter)]

    def z_copy(p, block, piece):
        at = (p * zs + block) * 2 + piece
        view = quarter_of(p, block, piece, core)
        device = (jnp.where(z < zs - 1, seq + groups, seq - groups), rep)
        return remote(view, view, z_ss.at[at], z_rs.at[at], device)

    def sib_copy(p, block, piece, part):
        at = (p * zs + block) * 2 + piece
        view = quarter_of(p, block, piece, part)
        return remote(view, view, sib_ss.at[at], sib_rs.at[at], peer(2 * y + 1 - core))

    def forward(n):
        p, block, piece = place(n)

        @pl.when(block == z)
        def _():
            for i in range(quarter_shards):
                source = (piece * 2 + core) * quarter_shards + i

                @pl.when(source != g)
                def _():
                    kv_copy(p, y, source).wait_recv()

        @pl.when(block != z)
        def _():
            z_copy(p, block, piece).wait_recv()

        @pl.when(z < zs - 1)
        def _():
            z_copy(p, block, piece).start()

        sib_copy(p, block, piece, core).start()

    def q_copy(p, d, row_of):
        return remote(
            q_out.at[p, d], q_mine.at[p, token_rows(row_of)],
            q_ss.at[p * groups + d], q_rs.at[p * groups + row_of], peer(d),
        )


    def slot_rows(i):
        return pl.ds(pl.multiple_of(i * SLOT_ROWS, SLOT_ROWS), SLOT_ROWS)

    def mid_copy(i):
        return remote(
            pages_out.at[slot_rows(xs + i)], pages_mid.at[slot_rows(i)],
            mid_ss.at[i], mid_rs.at[i], along_z(-hop, x),
        )

    def far_copy(i, x_from):
        origin_hi = jnp.where(z + hop < zs, z_hi, 1 - z_hi)
        return remote(
            pages_mid.at[slot_rows(i)], pages_ref.at[slot_rows(x_from * 2 + origin_hi)],
            far_ss.at[i], far_rs.at[x_from], along_z(-hop, i),
        )

    def x_copy(i, x_from):
        return remote(
            pages_out.at[slot_rows(i)], pages_ref.at[slot_rows(x_from * 2 + z_hi)],
            x_ss.at[i], x_rs.at[x_from], (seq, i * 2 + z_hi),
        )

    def pass_pages(i):
        mid_copy(i).wait_recv()
        far_copy(i, x).start()

    for i in range(xs):
        mid_copy(i).start()
    for i in both_ways(groups):
        q_copy(0, wrap(g + i, groups), g).start()
    forward(0)
    for i in range(1, xs):
        x_copy(wrap(x + i, xs), x).start()
    own_pages = pltpu.make_async_copy(
        pages_out.at[slot_rows(x)], pages_ref.at[slot_rows(rep)], local_sem.at[0]
    )
    own_pages.start()
    forward(1)
    for i in both_ways(groups):
        q_copy(1, wrap(g + i, groups), g).start()
    for n in range(2, 4):
        forward(n)

    @pl.when(units > 1)
    def _():
        for n in range(4, LEAD + 1):
            forward(n)

    def attend(p, block, piece, chunks, diagonal, first):
        keys_at = pl.ds(piece * half, half) if isinstance(piece, int) else pl.ds(
            pl.multiple_of(piece * half, half), half
        )
        keys = kv_all[p, block, keys_at, 0:HEAD]
        values = kv_all[p, block, keys_at, HEAD:2 * HEAD]
        extended = jnp.concatenate([values, jnp.ones((half, HEAD), jnp.bfloat16)], axis=1)
        for j in range(heads):
            for c in chunks:
                at = pl.ds(c * half, half)
                scores = lax.dot_general(
                    q_mine[p, at, j * HEAD:(j + 1) * HEAD], keys, NT,
                    preferred_element_type=jnp.float32,
                )
                if c == diagonal:
                    query_at = lax.broadcasted_iota(jnp.int32, (half, half), 0)
                    key_at = lax.broadcasted_iota(jnp.int32, (half, half), 1)
                    scores = jnp.where(key_at <= query_at, scores, -1e30)
                largest = jnp.max(scores, axis=1, keepdims=True)
                if first:
                    largest = jnp.broadcast_to(largest, (half, HEAD))
                else:
                    before = top[p, j, at, :]
                    largest = jnp.maximum(before, largest)
                    shrink = jnp.exp2((before - largest) * SCALE)
                top[p, j, at, :] = largest
                shift = jnp.concatenate([largest * SCALE] * max(1, half // HEAD), axis=1)[:, :half]
                weights = jnp.exp2(scores * SCALE - shift).astype(jnp.bfloat16)
                result = jnp.dot(weights, extended, preferred_element_type=jnp.float32)
                if not first:
                    result = acc[p, j, at, :] * jnp.concatenate([shrink, shrink], axis=1) + result
                acc[p, j, at, :] = result

    def o_columns(p, d):
        first = ((d // 2 * 2 + p) * 2 + lax.rem(d, 2)) * wide
        return o_ref.at[:, pl.ds(pl.multiple_of(first, wide), wide)]

    def o_copy(p, d, group_of):
        return remote(
            o_mine.at[p, token_rows(d)], o_columns(p, group_of),
            o_ss.at[p * groups + d], o_rs.at[p * groups + group_of], peer(d),
        )

    def own_rows(p):
        return pltpu.make_async_copy(
            o_mine.at[p, token_rows(g)], o_columns(p, g), local_sem.at[1 + p]
        )

    def finish(p, d):
        token = (z * groups + d) * tokens + lax.broadcasted_iota(jnp.int32, (tokens, HEAD), 0)
        for j in range(heads):
            total = acc[p, j, token_rows(d), :]
            result = total[:, 0:HEAD] / total[:, HEAD:2 * HEAD]
            o_mine[p, token_rows(d), j * HEAD:(j + 1) * HEAD] = jnp.where(
                token < length, result, 0.0
            ).astype(jnp.bfloat16)

    def step(i, carry):
        ahead = i + LEAD
        fresh = i >= 1
        for at in CATCH_UP:
            ahead = ahead - jnp.where(i >= at, 1, 0)
            fresh = fresh & (i != at)

        @pl.when(fresh & (ahead < 4 * units))
        def _():
            forward(ahead)

        n = i
        for known, order in ((units == 2, ORDER_TWO), (units > 2, ORDER_MORE)):
            for at, index in enumerate(order):
                n = jnp.where(known & (i == at), index, n)
        p, block, piece = place(n)
        sib_copy(p, block, piece, 1 - core).wait_recv()

        @pl.when((block == z) & (piece == 0))
        def _():
            for d in range(1, groups):
                source = wrap(g + d, groups)
                q_copy(p, source, source).wait_recv()
            attend(p, block, 0, (0, 1), 0, True)

        @pl.when((block == z) & (piece == 1))
        def _():
            attend(p, block, 1, (1,), 1, False)

        @pl.when(block != z)
        def _():
            attend(p, block, piece, (0, 1), None, False)

        @pl.when((block == 0) & (piece == 1))
        def _():
            for offset in both_ways(groups):
                d = wrap(g + offset, groups)
                finish(p, d)
                o_copy(p, d, g).start()
            finish(p, g)
            own_rows(p).start()

        for part in range(xs):
            @pl.when(i == PAGE_STEPS[part])
            def _():
                pass_pages(part)

        return carry

    lax.fori_loop(0, 4 * units, step, 0)

    for i in range(xs):
        @pl.when(PAGE_STEPS[i] >= 4 * units)
        def _():
            pass_pages(i)

    each_kv_send(lambda copy: copy.wait_send())
    for p in range(2):
        for i in range(1, groups):
            q_copy(p, wrap(g + i, groups), g).wait_send()
    for i in range(1, xs):
        other = wrap(x + i, xs)
        x_copy(other, x).wait_send()
        x_copy(other, other).wait_recv()
    for i in range(xs):
        mid_copy(i).wait_send()

    def sent(n, carry):
        p, block, piece = place(n)
        sib_copy(p, block, piece, core).wait_send()

        @pl.when(z < zs - 1)
        def _():
            z_copy(p, block, piece).wait_send()

        return carry

    lax.fori_loop(0, 4 * units, sent, 0)
    own_pages.wait()
    for p in range(2):
        own_rows(p).wait()
        for i in range(1, groups):
            d = wrap(g + i, groups)
            o_copy(p, d, g).wait_send()
            o_copy(p, d, d).wait_recv()
    for i in range(xs):
        far_copy(i, x).wait_send()
        far_copy(i, i).wait_recv()


def body(query_rows, unrotated_keys, value_projections, lengths, page_table):
    tokens, query_width = query_rows.shape[1:]
    groups = unrotated_keys.shape[2] // HEAD
    zs = lax.axis_size("seq") // groups
    owners = lax.axis_size("rep")
    xs = owners // Z_HALVES
    rows, wide = groups * tokens, query_width // (2 * groups)
    heads = wide // HEAD
    positions = lax.axis_index("seq") * tokens + jnp.arange(tokens, dtype=jnp.int32)
    cosine, sine = rotary_tables(positions)
    bf16, f32 = jnp.bfloat16, jnp.float32
    vmem = pl.BlockSpec(memory_space=pltpu.VMEM)
    smem = pl.BlockSpec(memory_space=pltpu.SMEM)
    dma = pltpu.SemaphoreType.DMA
    attended, pages = pl.pallas_call(
        functools.partial(kernel, groups, zs, xs),
        out_shape=(
            jax.ShapeDtypeStruct((tokens, query_width), bf16),
            jax.ShapeDtypeStruct((owners * SLOT_ROWS, 2 * groups * HEAD), bf16),
        ),
        in_specs=[vmem] * 5 + [smem] * 2,
        out_specs=(pl.BlockSpec(memory_space=pl.ANY),) * 2,
        scratch_shapes=[
            pltpu.VMEM((groups, tokens, 2 * HEAD), bf16),
            pltpu.VMEM((2, zs, rows, 2 * HEAD), bf16),
            pltpu.VMEM((2, groups, tokens, wide), bf16),
            pltpu.VMEM((2, rows, wide), bf16),
            pltpu.VMEM((2, rows, wide), bf16),
            pltpu.VMEM((2, heads, rows, 2 * HEAD), f32),
            pltpu.VMEM((2, heads, rows, HEAD), f32),
            pltpu.VMEM((owners * SLOT_ROWS, 2 * groups * HEAD), bf16),
            pltpu.VMEM((xs * SLOT_ROWS, 2 * groups * HEAD), bf16),
            dma((groups,)), dma((2 * groups,)), dma((2 * groups,)), dma((2 * groups,)),
            dma((2 * groups,)), dma((2 * groups,)), dma((4 * zs,)), dma((4 * zs,)),
            dma((4 * zs,)), dma((4 * zs,)),
            dma((xs,)), dma((xs,)), dma((xs,)), dma((xs,)), dma((xs,)), dma((xs,)),
            dma((3,)),
        ],
        compiler_params=pltpu.CompilerParams(
            collective_id=0, has_side_effects=True, vmem_limit_bytes=48 * 2**20
        ),
        name="recompute",
    )(
        query_rows[0], unrotated_keys[0], value_projections[0], cosine, sine, lengths,
        page_table[0, :, 0],
    )
    return (
        attended[None],
        pages.reshape(1, 1, owners, SLOTS, PAGE, 2 * groups * HEAD),
    )


def solution(mesh):
    return jax.shard_map(
        body,
        mesh=mesh,
        in_specs=(
            P("rep", "seq", None),
            P("rep", "seq", None),
            P("rep", "seq", None),
            P("rep"),
            P("rep", "seq", None),
        ),
        out_specs=(P("rep", "seq", None), P("rep", "seq", None, None, None, None)),
        check_vma=False,
    )
```

```python
import functools
import math

import jax
import jax.numpy as jnp
from jax import lax
from jax.experimental import pallas as pl
from jax.experimental.pallas import tpu as pltpu
from jax.sharding import PartitionSpec as P

HEAD = 128
PAGE = 8
SLOTS = 2
LEAD = 6
CATCH_UP = (5, 9, 13, 17, 21)
ORDER_TWO = (0, 1, 3, 4, 2, 5)
ORDER_MORE = (0, 1, 3, 4, 6, 7, 2, 5, 8)
PAGE_STEPS = (5, 9, 13, 17)
SLOT_ROWS = SLOTS * PAGE
Z_HALVES = 2
SCALE = math.log2(math.e) / math.sqrt(HEAD)
MESH = pl.DeviceIdType.MESH
NT = (((1,), (1,)), ((), ()))


def both_ways(n):
    first = [2, n - 2, 3, n - 1, n // 2, n // 2 + 1]
    return list(dict.fromkeys([i for i in first if 1 < i < n] + list(range(n - 1, 0, -1))))


def wrap(value, n):
    return jnp.where(value >= n, value - n, value)


def rotary_tables(token_positions):
    halfwidth = HEAD // 2
    frequency = jnp.exp(
        -jnp.arange(halfwidth, dtype=jnp.float32) * (2.0 * math.log(500000.0) / HEAD)
    )
    angles = token_positions.astype(jnp.float32)[:, None] * frequency[None, :]
    cosine, sine = jnp.cos(angles), jnp.sin(angles)
    return (
        jnp.concatenate([cosine, cosine], axis=-1),
        jnp.concatenate([-sine, sine], axis=-1),
    )


def kernel(
    groups, zs, xs,
    q_ref, k_ref, v_ref, cos_ref, sin_ref, len_ref, table_ref,
    o_ref, pages_ref,
    kv_out, kv_all, q_out, q_mine, o_mine, acc, top, pages_out, pages_mid,
    kv_ss, kv_rs, q_ss, q_rs, o_ss, o_rs, z_ss, z_rs, sib_ss, sib_rs, x_ss, x_rs,
    mid_ss, mid_rs, far_ss, far_rs, local_sem,
):
    tokens = q_ref.shape[0]
    rows = groups * tokens
    heads = q_ref.shape[1] // (2 * groups * HEAD)
    wide = heads * HEAD
    half = rows // 2
    quarter = rows // 4
    quarter_shards = groups // 4
    ys = groups // 2
    hop = zs // 2
    seq, rep = lax.axis_index("seq"), lax.axis_index("rep")
    z, g = seq // groups, lax.rem(seq, groups)
    y, core = g // 2, lax.rem(g, 2)
    my_core = lax.rem(g // quarter_shards, 2)
    x, z_hi = rep // 2, lax.rem(rep, 2)
    units = z + 1

    def peer(d):
        return (z * groups + d, rep)

    def along_z(shift, x_at):
        inside = (z + shift >= 0) & (z + shift < zs)
        step = jnp.where(inside, shift, jnp.where(z + shift < 0, shift + zs, shift - zs))
        return (seq + step * groups, x_at * 2 + jnp.where(inside, z_hi, 1 - z_hi))

    def remote(src, dst, ss, rs, device):
        return pltpu.make_async_remote_copy(
            src_ref=src, dst_ref=dst, send_sem=ss, recv_sem=rs,
            device_id=device, device_id_type=MESH,
        )

    def token_rows(d):
        return pl.ds(pl.multiple_of(d * tokens, tokens), tokens)

    barrier = pltpu.get_barrier_semaphore()

    def greet(device):
        pl.semaphore_signal(barrier, inc=1, device_id=device, device_id_type=MESH)

    for i in range(xs):
        greet(along_z(hop, i))
    for i in range(1, xs):
        greet((seq, wrap(x + i, xs) * 2 + z_hi))
    for i in range(1, groups):
        greet(peer(wrap(g + i, groups)))

    @pl.when(z > 0)
    def _():
        greet((seq - groups, rep))

    cosine, sine = cos_ref[...], sin_ref[...]

    def rotate(head):
        head = head.astype(jnp.float32)
        return (head * cosine + pltpu.roll(head, HEAD // 2, axis=1) * sine).astype(jnp.bfloat16)

    for d in range(groups):
        kv_out[d, :, 0:HEAD] = rotate(k_ref[:, d * HEAD:(d + 1) * HEAD])
        kv_out[d, :, HEAD:2 * HEAD] = v_ref[:, d * HEAD:(d + 1) * HEAD]

    @pl.when(my_core == core)
    def _():
        for p in range(2):
            kv_all[p, z, token_rows(g), :] = kv_out[2 * y + p]

    length = len_ref[0]
    owners = [table_ref[j] for j in range(tokens // PAGE)]
    lane = lax.broadcasted_iota(jnp.int32, (1, tokens), 1)
    target = jnp.full((1, tokens), -1, jnp.int32)
    for j, owner in enumerate(owners):
        earlier = jnp.int32(0)
        for i in range(j):
            earlier = earlier + jnp.where(owners[i] == owner, 1, 0)
        owner_x = owner >> 1
        other = jnp.where((owner & 1) == z_hi, 0, xs)
        base = (other + owner_x) * SLOT_ROWS + earlier * PAGE - j * PAGE
        target = jnp.where(
            (lane >= j * PAGE) & (lane < (j + 1) * PAGE) & (earlier < SLOTS), lane + base, target
        )
    target = jnp.where(seq * tokens + lane < length, target, -1)
    slot = lax.broadcasted_iota(jnp.int32, (2 * xs * SLOT_ROWS, tokens), 0)
    chosen = jnp.where(slot == target, 1.0, 0.0).astype(jnp.bfloat16)
    for d in range(groups):
        for part in range(2):
            column = (part * groups + d) * HEAD
            pages_out[:, column:column + HEAD] = jnp.dot(
                chosen, kv_out[d, :, part * HEAD:(part + 1) * HEAD],
                preferred_element_type=jnp.float32,
            ).astype(jnp.bfloat16)

    def rotate_queries(p, d):
        first = ((d // 2 * 2 + p) * 2 + lax.rem(d, 2)) * wide
        for j in range(heads):
            columns = pl.ds(pl.multiple_of(first + j * HEAD, HEAD), HEAD)
            q_out[p, d, :, j * HEAD:(j + 1) * HEAD] = rotate(q_ref[:, columns])

    for p in range(2):
        def one(d, carry):
            rotate_queries(p, d)
            return carry

        lax.fori_loop(0, groups, one, 0)
        q_mine[p, token_rows(g), :] = q_out[p, g]

    partners = (groups - 1) + (xs - 1) + xs
    pl.semaphore_wait(barrier, partners + jnp.where(z < zs - 1, 1, 0))

    def kv_copy(p, y_to, row_of):
        return remote(
            kv_out.at[2 * y_to + p], kv_all.at[p, z, token_rows(row_of)],
            kv_ss.at[p * ys + y_to], kv_rs.at[p * groups + row_of],
            peer(2 * y_to + lax.rem(row_of // quarter_shards, 2)),
        )

    def each_kv_send(act):
        for p in range(2):
            for i in sorted(range(1, ys), key=lambda i: abs(i - ys / 2), reverse=True):
                act(kv_copy(p, wrap(y + i, ys), g))

            @pl.when(my_core != core)
            def _():
                act(kv_copy(p, y, g))

    each_kv_send(lambda copy: copy.start())

    def place(n):
        late = n >= 3 * units
        t = jnp.where(late, n - 3 * units, n // 3)
        kind = jnp.where(late, 3, n - 3 * t)
        return kind // 2, z - t, lax.rem(kind, 2)

    def quarter_of(p, block, piece, part):
        first = (piece * 2 + part) * quarter
        return kv_all.at[p, block, pl.ds(pl.multiple_of(first, quarter), quarter)]

    def z_copy(p, block, piece):
        at = (p * zs + block) * 2 + piece
        view = quarter_of(p, block, piece, core)
        device = (jnp.where(z < zs - 1, seq + groups, seq - groups), rep)
        return remote(view, view, z_ss.at[at], z_rs.at[at], device)

    def sib_copy(p, block, piece, part):
        at = (p * zs + block) * 2 + piece
        view = quarter_of(p, block, piece, part)
        return remote(view, view, sib_ss.at[at], sib_rs.at[at], peer(2 * y + 1 - core))

    def forward(n):
        p, block, piece = place(n)

        @pl.when(block == z)
        def _():
            for i in range(quarter_shards):
                source = (piece * 2 + core) * quarter_shards + i

                @pl.when(source != g)
                def _():
                    kv_copy(p, y, source).wait_recv()

        @pl.when(block != z)
        def _():
            z_copy(p, block, piece).wait_recv()

        @pl.when(z < zs - 1)
        def _():
            z_copy(p, block, piece).start()

        sib_copy(p, block, piece, core).start()

    def q_copy(p, d, row_of):
        return remote(
            q_out.at[p, d], q_mine.at[p, token_rows(row_of)],
            q_ss.at[p * groups + d], q_rs.at[p * groups + row_of], peer(d),
        )


    def slot_rows(i):
        return pl.ds(pl.multiple_of(i * SLOT_ROWS, SLOT_ROWS), SLOT_ROWS)

    def mid_copy(i):
        return remote(
            pages_out.at[slot_rows(xs + i)], pages_mid.at[slot_rows(i)],
            mid_ss.at[i], mid_rs.at[i], along_z(-hop, x),
        )

    def far_copy(i, x_from):
        origin_hi = jnp.where(z + hop < zs, z_hi, 1 - z_hi)
        return remote(
            pages_mid.at[slot_rows(i)], pages_ref.at[slot_rows(x_from * 2 + origin_hi)],
            far_ss.at[i], far_rs.at[x_from], along_z(-hop, i),
        )

    def x_copy(i, x_from):
        return remote(
            pages_out.at[slot_rows(i)], pages_ref.at[slot_rows(x_from * 2 + z_hi)],
            x_ss.at[i], x_rs.at[x_from], (seq, i * 2 + z_hi),
        )

    def pass_pages(i):
        mid_copy(i).wait_recv()
        far_copy(i, x).start()

    for i in range(xs):
        mid_copy(i).start()
    for i in both_ways(groups):
        q_copy(0, wrap(g + i, groups), g).start()
    forward(0)
    for i in range(1, xs):
        x_copy(wrap(x + i, xs), x).start()
    own_pages = pltpu.make_async_copy(
        pages_out.at[slot_rows(x)], pages_ref.at[slot_rows(rep)], local_sem.at[0]
    )
    own_pages.start()
    forward(1)
    for i in both_ways(groups):
        q_copy(1, wrap(g + i, groups), g).start()
    for n in range(2, 4):
        forward(n)

    @pl.when(units > 1)
    def _():
        for n in range(4, LEAD + 1):
            forward(n)

    def attend(p, block, piece, chunks, diagonal, first):
        keys_at = pl.ds(piece * half, half) if isinstance(piece, int) else pl.ds(
            pl.multiple_of(piece * half, half), half
        )
        keys = kv_all[p, block, keys_at, 0:HEAD]
        values = kv_all[p, block, keys_at, HEAD:2 * HEAD]
        extended = jnp.concatenate([values, jnp.ones((half, HEAD), jnp.bfloat16)], axis=1)
        for j in range(heads):
            for c in chunks:
                at = pl.ds(c * half, half)
                scores = lax.dot_general(
                    q_mine[p, at, j * HEAD:(j + 1) * HEAD], keys, NT,
                    preferred_element_type=jnp.float32,
                )
                if c == diagonal:
                    query_at = lax.broadcasted_iota(jnp.int32, (half, half), 0)
                    key_at = lax.broadcasted_iota(jnp.int32, (half, half), 1)
                    scores = jnp.where(key_at <= query_at, scores, -1e30)
                largest = jnp.max(scores, axis=1, keepdims=True)
                if first:
                    largest = jnp.broadcast_to(largest, (half, HEAD))
                else:
                    before = top[p, j, at, :]
                    largest = jnp.maximum(before, largest)
                    shrink = jnp.exp2((before - largest) * SCALE)
                top[p, j, at, :] = largest
                shift = jnp.concatenate([largest * SCALE] * max(1, half // HEAD), axis=1)[:, :half]
                weights = jnp.exp2(scores * SCALE - shift).astype(jnp.bfloat16)
                result = jnp.dot(weights, extended, preferred_element_type=jnp.float32)
                if not first:
                    result = acc[p, j, at, :] * jnp.concatenate([shrink, shrink], axis=1) + result
                acc[p, j, at, :] = result

    def o_columns(p, d):
        first = ((d // 2 * 2 + p) * 2 + lax.rem(d, 2)) * wide
        return o_ref.at[:, pl.ds(pl.multiple_of(first, wide), wide)]

    def o_copy(p, d, group_of):
        return remote(
            o_mine.at[p, token_rows(d)], o_columns(p, group_of),
            o_ss.at[p * groups + d], o_rs.at[p * groups + group_of], peer(d),
        )

    def own_rows(p):
        return pltpu.make_async_copy(
            o_mine.at[p, token_rows(g)], o_columns(p, g), local_sem.at[1 + p]
        )

    def finish(p, d):
        token = (z * groups + d) * tokens + lax.broadcasted_iota(jnp.int32, (tokens, HEAD), 0)
        for j in range(heads):
            total = acc[p, j, token_rows(d), :]
            result = total[:, 0:HEAD] / total[:, HEAD:2 * HEAD]
            o_mine[p, token_rows(d), j * HEAD:(j + 1) * HEAD] = jnp.where(
                token < length, result, 0.0
            ).astype(jnp.bfloat16)

    def step(i, carry):
        ahead = i + LEAD
        fresh = i >= 1
        for at in CATCH_UP:
            ahead = ahead - jnp.where(i >= at, 1, 0)
            fresh = fresh & (i != at)

        @pl.when(fresh & (ahead < 4 * units))
        def _():
            forward(ahead)

        n = i
        for known, order in ((units == 2, ORDER_TWO), (units > 2, ORDER_MORE)):
            for at, index in enumerate(order):
                n = jnp.where(known & (i == at), index, n)
        p, block, piece = place(n)
        sib_copy(p, block, piece, 1 - core).wait_recv()

        @pl.when((block == z) & (piece == 0))
        def _():
            for d in range(1, groups):
                source = wrap(g + d, groups)
                q_copy(p, source, source).wait_recv()
            attend(p, block, 0, (0, 1), 0, True)

        @pl.when((block == z) & (piece == 1))
        def _():
            attend(p, block, 1, (1,), 1, False)

        @pl.when(block != z)
        def _():
            attend(p, block, piece, (0, 1), None, False)

        @pl.when((block == 0) & (piece == 1))
        def _():
            for offset in both_ways(groups):
                d = wrap(g + offset, groups)
                finish(p, d)
                o_copy(p, d, g).start()
            finish(p, g)
            own_rows(p).start()

        for part in range(xs):
            @pl.when(i == PAGE_STEPS[part])
            def _():
                pass_pages(part)

        return carry

    lax.fori_loop(0, 4 * units, step, 0)

    for i in range(xs):
        @pl.when(PAGE_STEPS[i] >= 4 * units)
        def _():
            pass_pages(i)

    each_kv_send(lambda copy: copy.wait_send())
    for p in range(2):
        for i in range(1, groups):
            q_copy(p, wrap(g + i, groups), g).wait_send()
    for i in range(1, xs):
        other = wrap(x + i, xs)
        x_copy(other, x).wait_send()
        x_copy(other, other).wait_recv()
    for i in range(xs):
        mid_copy(i).wait_send()

    def sent(n, carry):
        p, block, piece = place(n)
        sib_copy(p, block, piece, core).wait_send()

        @pl.when(z < zs - 1)
        def _():
            z_copy(p, block, piece).wait_send()

        return carry

    lax.fori_loop(0, 4 * units, sent, 0)
    own_pages.wait()
    for p in range(2):
        own_rows(p).wait()
        for i in range(1, groups):
            d = wrap(g + i, groups)
            o_copy(p, d, g).wait_send()
            o_copy(p, d, d).wait_recv()
    for i in range(xs):
        far_copy(i, x).wait_send()
        far_copy(i, i).wait_recv()


def body(query_rows, unrotated_keys, value_projections, lengths, page_table):
    tokens, query_width = query_rows.shape[1:]
    groups = unrotated_keys.shape[2] // HEAD
    zs = lax.axis_size("seq") // groups
    owners = lax.axis_size("rep")
    xs = owners // Z_HALVES
    rows, wide = groups * tokens, query_width // (2 * groups)
    heads = wide // HEAD
    positions = lax.axis_index("seq") * tokens + jnp.arange(tokens, dtype=jnp.int32)
    cosine, sine = rotary_tables(positions)
    bf16, f32 = jnp.bfloat16, jnp.float32
    vmem = pl.BlockSpec(memory_space=pltpu.VMEM)
    smem = pl.BlockSpec(memory_space=pltpu.SMEM)
    dma = pltpu.SemaphoreType.DMA
    attended, pages = pl.pallas_call(
        functools.partial(kernel, groups, zs, xs),
        out_shape=(
            jax.ShapeDtypeStruct((tokens, query_width), bf16),
            jax.ShapeDtypeStruct((owners * SLOT_ROWS, 2 * groups * HEAD), bf16),
        ),
        in_specs=[vmem] * 5 + [smem] * 2,
        out_specs=(pl.BlockSpec(memory_space=pl.ANY),) * 2,
        scratch_shapes=[
            pltpu.VMEM((groups, tokens, 2 * HEAD), bf16),
            pltpu.VMEM((2, zs, rows, 2 * HEAD), bf16),
            pltpu.VMEM((2, groups, tokens, wide), bf16),
            pltpu.VMEM((2, rows, wide), bf16),
            pltpu.VMEM((2, rows, wide), bf16),
            pltpu.VMEM((2, heads, rows, 2 * HEAD), f32),
            pltpu.VMEM((2, heads, rows, HEAD), f32),
            pltpu.VMEM((owners * SLOT_ROWS, 2 * groups * HEAD), bf16),
            pltpu.VMEM((xs * SLOT_ROWS, 2 * groups * HEAD), bf16),
            dma((groups,)), dma((2 * groups,)), dma((2 * groups,)), dma((2 * groups,)),
            dma((2 * groups,)), dma((2 * groups,)), dma((4 * zs,)), dma((4 * zs,)),
            dma((4 * zs,)), dma((4 * zs,)),
            dma((xs,)), dma((xs,)), dma((xs,)), dma((xs,)), dma((xs,)), dma((xs,)),
            dma((3,)),
        ],
        compiler_params=pltpu.CompilerParams(
            collective_id=0, has_side_effects=True, vmem_limit_bytes=48 * 2**20
        ),
        name="recompute",
    )(
        query_rows[0], unrotated_keys[0], value_projections[0], cosine, sine, lengths,
        page_table[0, :, 0],
    )
    return (
        attended[None],
        pages.reshape(1, 1, owners, SLOTS, PAGE, 2 * groups * HEAD),
    )


def solution(mesh):
    return jax.shard_map(
        body,
        mesh=mesh,
        in_specs=(
            P("rep", "seq", None),
            P("rep", "seq", None),
            P("rep", "seq", None),
            P("rep"),
            P("rep", "seq", None),
        ),
        out_specs=(P("rep", "seq", None), P("rep", "seq", None, None, None, None)),
        check_vma=False,
    )
```
